256 devices in a mesh: fibre: 16 (over z, core), rest: 16 (over x, y).
Axes of the slice: x: 4, y: 4, z: 8, core: 2. Of those that a mesh axis runs over, the one named last changes fastest.
Arguments:
- slab: float32 [672, 262144], P('fibre', 'rest'), may hold values from -6 to 6
- start_basis: float32 [672, 96], replicated, may hold values from -6 to 6
Outputs:
- factor: float32 [672, 96], replicated
- core: float32 [96, 262144], P('fibre', 'rest')
The draws below stay inside these ranges and needn't reach their ends.
All inputs are finite; a program needn't handle non-finite values.
Results may differ from the reference program's by a relative error of at most 0.00023.
Values sent between devices are 32-bit elements; how exact they have to be, the bound alone decides.
A program may use at most 64 MiB of HBM per device.

```python
import jax
import jax.numpy as jnp
from jax import lax

I1 = 672
RANK = 96
ITERS = 3
COLS = 262144


def block_levels(key, shape, split, smallest, top_value):
    gain = 1.0
    for axis_at, shards_of in split:
        draws = jax.random.uniform(jax.random.fold_in(jax.random.fold_in(key, 6), axis_at), (shards_of,), jnp.float32, smallest / len(split), top_value / len(split))
        gain = gain * jnp.repeat(jnp.exp(draws), shape[axis_at] // shards_of).reshape((-1,) + (1,) * (len(shape) - 1 - axis_at))
    return gain


def gaussian(own_key, dims, scale, reach, pieces=(), dtype=jnp.bfloat16):
    result = jax.random.normal(own_key, dims, jnp.float32) * scale
    if len(pieces) > 0:
        result = block_levels(own_key, dims, pieces, -0.22, 0.18) * result
    return jnp.clip(result, min=-reach, max=reach).astype(dtype)


def setup_inputs(seed: int = 0) -> dict:
    key_of = jax.random.split(jax.random.key(seed), 3)
    slab = gaussian(key_of[0], (I1, COLS), 1.0, 6.0, ((0, 16), (1, 16)), jnp.float32)
    start_basis = gaussian(key_of[1], (I1, RANK), 1.0, 6.0, (), jnp.float32)
    return {"slab": slab, "start_basis": start_basis}


def reference(slab, start_basis):
    hp = lax.Precision.HIGHEST
    gram = jnp.dot(slab.astype(jnp.float32), slab.T.astype(jnp.float32), precision=hp, preferred_element_type=jnp.float32)
    basis = start_basis
    for step in range(ITERS):
        image = jnp.dot(gram.astype(jnp.float32), basis.astype(jnp.float32), precision=hp, preferred_element_type=jnp.float32)
        small = jnp.dot(image.T.astype(jnp.float32), image.astype(jnp.float32), precision=hp, preferred_element_type=jnp.float32)
        lower = jnp.linalg.cholesky(small)
        basis = lax.linalg.triangular_solve(lower, image, left_side=False, lower=True, transpose_a=True)
    core = jnp.dot(basis.T.astype(jnp.float32), slab.astype(jnp.float32), precision=hp, preferred_element_type=jnp.float32)
    return (basis, core)
```

```python
import jax
import jax.numpy as jnp
from jax import lax
from jax.experimental import pallas as pl
from jax.experimental.pallas import tpu as pltpu
from jax.sharding import PartitionSpec as P

ITERS = 3
HP = lax.Precision.HIGHEST
F32 = jnp.float32
BF16 = jnp.bfloat16
NF = 16
NR = 16
NZ = 8
ROWS = 42
I1 = 672
PAD1 = 768
RANK = 96
COLS = 16384
OWN = 1024
CHUNKS = 4
CW = OWN // CHUNKS
VMEM_LIMIT = 56 * 1024 * 1024

NT = (((1,), (1,)), ((), ()))
NN = (((1,), (0,)), ((), ()))


def split(x):
    hi = x.astype(BF16)
    lo = (x - hi.astype(F32)).astype(BF16)
    return hi, lo


def dot3(a, b, dims):
    ah, al = a
    bh, bl = b

    def d(u, v):
        return lax.dot_general(u, v, dims, preferred_element_type=F32)

    return d(ah, bh) + (d(ah, bl) + d(al, bh))


def remote(src, dst, send, recv, device):
    return pltpu.make_async_remote_copy(
        src_ref=src, dst_ref=dst, send_sem=send, recv_sem=recv,
        device_id=device, device_id_type=pl.DeviceIdType.MESH,
    )


def wrap(v, n):
    return lax.rem(v + n, n)


OFF_DIAG = [(i, j) for i in range(5) for j in range(i)]


def gram_kernel(slab, f_out, g_out, got, fc, acc, part, ra, sa, rb, own, rc, mine, full,
                s_own, s_x, r_x, s_a, r_a, s_b, r_b, s_c, r_c, s_d, r_d, s_e, r_e, s_f, r_f, s_o, s_g):
    f = lax.axis_index("fibre")
    r = lax.axis_index("rest")
    z = f // 2
    c = lax.rem(f, 2)
    other = z * 2 + (1 - c)

    barrier = pltpu.get_barrier_semaphore()
    for d in range(1, NF):
        pl.semaphore_signal(barrier, inc=1, device_id={"fibre": wrap(f + d, NF)}, device_id_type=pl.DeviceIdType.MESH)
    for d in range(1, NR):
        pl.semaphore_signal(barrier, inc=1, device_id={"rest": wrap(r + d, NR)}, device_id_type=pl.DeviceIdType.MESH)

    own_copy = pltpu.make_async_copy(slab.at[:, pl.ds(pl.multiple_of(f * OWN, OWN), OWN)], got.at[f], s_own)
    own_copy.start()
    pl.semaphore_wait(barrier, NF - 1 + NR - 1)

    def x_copy(ch, d):
        to = wrap(f + d, NF)
        return remote(
            slab.at[:, pl.ds(pl.multiple_of(to * OWN + ch * CW, CW), CW)],
            got.at[f, :, pl.ds(ch * CW, CW)],
            s_x.at[ch, d], r_x.at[ch, d], {"fibre": to},
        )

    for ch in range(CHUNKS):
        for d in range(1, NF):
            x_copy(ch, d).start()
    fc[pl.ds(I1, PAD1 - I1), :] = jnp.zeros((PAD1 - I1, OWN), F32)
    own_copy.wait()
    for ch in range(CHUNKS):
        for d in range(1, NF):
            x_copy(ch, d).wait_recv()
        cols = pl.ds(ch * CW, CW)
        for s in range(NF):
            fc[pl.ds(s * ROWS, ROWS), cols] = got[s, :, cols]
        hi, lo = split(fc[:, cols])
        for k in range(3):
            top, wide = k * 256, (k + 1) * 256
            new = dot3((hi[top:top + 256], lo[top:top + 256]), (hi[:wide], lo[:wide]), NT)
            if ch == 0:
                acc[pl.ds(top, 256), pl.ds(0, wide)] = new
            else:
                acc[pl.ds(top, 256), pl.ds(0, wide)] += new
    f_copy = pltpu.make_async_copy(fc.at[pl.ds(0, I1), :], f_out, s_o)
    f_copy.start()

    def put(b, value):
        part[b // 8, pl.ds((2 * b) % 16, 2)] = value.reshape(2, 8, 8, 128)

    def blk(i, j, rows=128):
        return acc[pl.ds(i * 128, rows), pl.ds(j * 128, 128)]

    row_id = lax.broadcasted_iota(jnp.int32, (128, 128), 0)
    col_id = lax.broadcasted_iota(jnp.int32, (128, 128), 1)
    for b, (i, j) in enumerate(OFF_DIAG):
        put(b, blk(i, j))
    second = blk(1, 1)
    put(10, jnp.where(row_id >= col_id, blk(0, 0), second))
    for k in range(2, 5):
        put(9 + k, blk(k, k))
    put(14, jnp.concatenate([blk(5, j, 32) for j in range(4)], axis=0))
    diagonal = jnp.sum(jnp.where(row_id == col_id, second, 0.0), axis=0, keepdims=True)
    put(15, jnp.concatenate(
        [blk(5, 4, 32), blk(5, 5, 32), jnp.broadcast_to(diagonal, (8, 128)), jnp.zeros((56, 128), F32)], axis=0))

    a_copy = remote(part.at[1 - c], ra, s_a, r_a, {"fibre": other})
    a_copy.start()
    a_copy.wait_recv()
    sa[...] = part[c] + ra[...]

    def b_copy(d):
        to = wrap(r + d, NR)
        return remote(sa.at[to], rb.at[d], s_b.at[d], r_b.at[d], {"rest": to})

    for d in range(1, NR):
        b_copy(d).start()
    total = sa[r]
    for d in range(1, NR):
        b_copy(d).wait_recv()
        total = total + rb[d]
    own[...] = total

    def c_copy(d):
        to = wrap(z + d, NZ)
        return remote(own.at[to], rc.at[d], s_c.at[d], r_c.at[d], {"fibre": to * 2 + c})

    for d in range(1, NZ):
        c_copy(d).start()
    tile = own[z]
    for d in range(1, NZ):
        c_copy(d).wait_recv()
        tile = tile + rc[d]
    mine[...] = tile
    full[c, r, z] = tile

    def d_copy(d):
        return remote(mine, full.at[c, r, z], s_d.at[d], r_d.at[d], {"fibre": wrap(z + d, NZ) * 2 + c})

    for d in range(1, NZ):
        d_copy(d).start()
    for d in range(1, NZ):
        d_copy(d).wait_recv()

    def e_copy(d):
        return remote(full.at[c, r], full.at[c, r], s_e.at[d], r_e.at[d], {"rest": wrap(r + d, NR)})

    def f_pass(d):
        at = wrap(r - d, NR)
        return remote(full.at[c, at], full.at[c, at], s_f.at[d], r_f.at[d], {"fibre": other})

    for d in range(1, NR):
        e_copy(d).start()
    f_pass(0).start()
    for d in range(1, NR):
        e_copy(d).wait_recv()
        f_pass(d).start()
    for d in range(NR):
        f_pass(d).wait_recv()
    g_copy = pltpu.make_async_copy(full, g_out, s_g)
    g_copy.start()

    for ch in range(CHUNKS):
        for d in range(1, NF):
            x_copy(ch, d).wait_send()
    a_copy.wait_send()
    for d in range(1, NR):
        b_copy(d).wait_send()
    for d in range(1, NZ):
        c_copy(d).wait_send()
        d_copy(d).wait_send()
    for d in range(1, NR):
        e_copy(d).wait_send()
    for d in range(NR):
        f_pass(d).wait_send()
    f_copy.wait()
    g_copy.wait()


def gram_call(slab):
    dma = pltpu.SemaphoreType.DMA
    any_spec = pl.BlockSpec(memory_space=pl.ANY)
    return pl.pallas_call(
        gram_kernel,
        out_shape=(
            jax.ShapeDtypeStruct((I1, OWN), F32),
            jax.ShapeDtypeStruct((2, NR, NZ, 8, 128), F32),
        ),
        in_specs=[any_spec],
        out_specs=(any_spec, any_spec),
        scratch_shapes=[
            pltpu.VMEM((NF, ROWS, OWN), F32),
            pltpu.VMEM((PAD1, OWN), F32),
            pltpu.VMEM((PAD1, PAD1), F32),
            pltpu.VMEM((2, NR, NZ, 8, 128), F32),
            pltpu.VMEM((NR, NZ, 8, 128), F32),
            pltpu.VMEM((NR, NZ, 8, 128), F32),
            pltpu.VMEM((NR, NZ, 8, 128), F32),
            pltpu.VMEM((NZ, 8, 128), F32),
            pltpu.VMEM((NZ, 8, 128), F32),
            pltpu.VMEM((8, 128), F32),
            pltpu.VMEM((2, NR, NZ, 8, 128), F32),
            dma,
            dma((CHUNKS, NF)), dma((CHUNKS, NF)),
            dma, dma,
            dma((NR,)), dma((NR,)),
            dma((NZ,)), dma((NZ,)),
            dma((NZ,)), dma((NZ,)),
            dma((NR,)), dma((NR,)),
            dma((NR,)), dma((NR,)),
            dma, dma,
        ],
        compiler_params=pltpu.CompilerParams(
            collective_id=0, has_side_effects=True, vmem_limit_bytes=VMEM_LIMIT),
        name="gram",
    )(slab)


def inverse_factor(small):
    tiles = [small[8 * t:8 * t + 8] for t in range(RANK // 8)]
    lane = lax.broadcasted_iota(jnp.int32, (8, 128), 1)
    sub = lax.broadcasted_iota(jnp.int32, (8, 128), 0)
    pivots = [jnp.ones((8, 128), F32) for _ in tiles]
    for j in range(RANK):
        t, i = divmod(j, 8)
        row = jnp.broadcast_to(tiles[t][i:i + 1, :], (8, 128))
        pivot = jnp.broadcast_to(row[:, j:j + 1], (8, 128))
        pivots[t] = jnp.where(sub == i, pivot, pivots[t])
        scaled = jnp.where(lane == j, 1.0, row) / pivot
        for k in range(t, len(tiles)):
            times = jnp.broadcast_to(tiles[k][:, j:j + 1], (8, 128))
            new = jnp.where(lane == j, 0.0, tiles[k]) - times * scaled
            if k == t:
                kept = jnp.where(lane == j, 1.0, tiles[k])
                new = jnp.where(sub > i, new, jnp.where(sub == i, kept, tiles[k]))
            tiles[k] = new
    tiles = [u * lax.rsqrt(p) for u, p in zip(tiles, pivots)]
    tiles = [jnp.where(lane <= sub + 8 * t, u, 0.0) for t, u in enumerate(tiles)]
    return jnp.concatenate(tiles, axis=0)


def iterate_kernel(g, start, fibres, factor, core, gh, gl, basis, fh, fl):
    row_id = lax.broadcasted_iota(jnp.int32, (128, 128), 0)
    col_id = lax.broadcasted_iota(jnp.int32, (128, 128), 1)

    def get(b):
        return g[b // 8, pl.ds((2 * b) % 16, 2)].reshape(128, 128)

    def store(i, j, value):
        hi, lo = split(value)
        at = (pl.ds(i * 128, 128), pl.ds(j * 128, 128))
        gh[at] = hi
        gl[at] = lo

    for b, (i, j) in enumerate(OFF_DIAG):
        value = get(b)
        store(i, j, value)
        store(j, i, value.T)
    for k in range(2, 5):
        store(k, k, get(9 + k))
    last = get(15)
    both = get(10)
    flip = both.T
    store(0, 0, jnp.where(row_id >= col_id, both, flip))
    diagonal = jnp.broadcast_to(last[64:65], (128, 128))
    store(1, 1, jnp.where(row_id < col_id, both, jnp.where(row_id > col_id, flip, diagonal)))
    most = get(14)
    strips = [most[32 * k:32 * k + 32] for k in range(4)] + [last[0:32], last[32:64]]
    for j, strip in enumerate(strips):
        value = jnp.concatenate([strip, jnp.zeros((96, 128), F32)], axis=0)
        store(5, j, value)
        if j < 5:
            store(j, 5, value.T)

    fh[...], fl[...] = split(fibres[...])
    basis[...] = jnp.concatenate([start[...], jnp.zeros((PAD1 - I1, RANK), F32)], axis=0).T

    def step(_, carry):
        image = dot3(split(basis[...]), (gh[...], gl[...]), NN)
        wide = jnp.concatenate([image, jnp.zeros((128 - RANK, PAD1), F32)], axis=0)
        small = lax.dot_general(image, wide, NT, precision=HP, preferred_element_type=F32)
        inverse = inverse_factor(small)[:, :RANK]
        basis[...] = lax.dot_general(inverse, image, NN, precision=HP, preferred_element_type=F32)
        return carry

    lax.fori_loop(0, ITERS, step, 0)
    last_basis = basis[...]
    factor[...] = last_basis.T[:I1]
    product = dot3(split(last_basis[:, :I1]), (fh[...], fl[...]), NN)
    for j in range(NF):
        core[j] = product[6 * j:6 * j + 6]


def iterate_call(g, start, fibres):
    vmem = pl.BlockSpec(memory_space=pltpu.VMEM)
    return pl.pallas_call(
        iterate_kernel,
        out_shape=(
            jax.ShapeDtypeStruct((I1, RANK), F32),
            jax.ShapeDtypeStruct((NF, RANK // NF, OWN), F32),
        ),
        in_specs=[vmem, vmem, vmem],
        out_specs=(vmem, vmem),
        scratch_shapes=[
            pltpu.VMEM((PAD1, PAD1), BF16),
            pltpu.VMEM((PAD1, PAD1), BF16),
            pltpu.VMEM((RANK, PAD1), F32),
            pltpu.VMEM((I1, OWN), BF16),
            pltpu.VMEM((I1, OWN), BF16),
        ],
        compiler_params=pltpu.CompilerParams(vmem_limit_bytes=VMEM_LIMIT),
        name="iterate",
    )(g, start, fibres)


def core_kernel(blocks, out, s_own, s_x, r_x):
    f = lax.axis_index("fibre")
    barrier = pltpu.get_barrier_semaphore()
    for d in range(1, NF):
        pl.semaphore_signal(barrier, inc=1, device_id={"fibre": wrap(f + d, NF)}, device_id_type=pl.DeviceIdType.MESH)
    at = pl.ds(pl.multiple_of(f * OWN, OWN), OWN)
    own_copy = pltpu.make_async_copy(blocks.at[f], out.at[:, at], s_own)
    own_copy.start()
    pl.semaphore_wait(barrier, NF - 1)

    def copy(d):
        to = wrap(f + d, NF)
        return remote(blocks.at[to], out.at[:, at], s_x.at[d], r_x.at[d], {"fibre": to})

    for d in range(1, NF):
        copy(d).start()
    own_copy.wait()
    for d in range(1, NF):
        copy(d).wait()


def core_call(blocks):
    dma = pltpu.SemaphoreType.DMA
    any_spec = pl.BlockSpec(memory_space=pl.ANY)
    return pl.pallas_call(
        core_kernel,
        out_shape=jax.ShapeDtypeStruct((RANK // NF, COLS), F32),
        in_specs=[any_spec],
        out_specs=any_spec,
        scratch_shapes=[dma, dma((NF,)), dma((NF,))],
        compiler_params=pltpu.CompilerParams(
            collective_id=1, has_side_effects=True, vmem_limit_bytes=VMEM_LIMIT),
        name="core",
    )(blocks)


def shards(slab, start_basis):
    fibres, gram = gram_call(slab)
    factor, blocks = iterate_call(gram, start_basis, fibres)
    return factor, core_call(blocks)


def solution(mesh):
    return jax.shard_map(
        shards,
        mesh=mesh,
        in_specs=(P("fibre", "rest"), P()),
        out_specs=(P(), P("fibre", "rest")),
        check_vma=False,
    )
```

```python
import jax
import jax.numpy as jnp
from jax import lax
from jax.experimental import pallas as pl
from jax.experimental.pallas import tpu as pltpu
from jax.sharding import PartitionSpec as P

ITERS = 3
HP = lax.Precision.HIGHEST
F32 = jnp.float32
BF16 = jnp.bfloat16
NF = 16
NR = 16
NZ = 8
ROWS = 42
I1 = 672
PAD1 = 768
RANK = 96
COLS = 16384
OWN = 1024
CHUNKS = 4
CW = OWN // CHUNKS
VMEM_LIMIT = 56 * 1024 * 1024

NT = (((1,), (1,)), ((), ()))
NN = (((1,), (0,)), ((), ()))


def split(x):
    hi = x.astype(BF16)
    lo = (x - hi.astype(F32)).astype(BF16)
    return hi, lo


def dot3(a, b, dims):
    ah, al = a
    bh, bl = b

    def d(u, v):
        return lax.dot_general(u, v, dims, preferred_element_type=F32)

    return d(ah, bh) + (d(ah, bl) + d(al, bh))


def remote(src, dst, send, recv, device):
    return pltpu.make_async_remote_copy(
        src_ref=src, dst_ref=dst, send_sem=send, recv_sem=recv,
        device_id=device, device_id_type=pl.DeviceIdType.MESH,
    )


def wrap(v, n):
    return lax.rem(v + n, n)


OFF_DIAG = [(i, j) for i in range(5) for j in range(i)]


def gram_kernel(slab, f_out, g_out, got, fc, acc, part, ra, sa, rb, own, rc, mine, full,
                s_own, s_x, r_x, s_a, r_a, s_b, r_b, s_c, r_c, s_d, r_d, s_e, r_e, s_f, r_f, s_o, s_g):
    f = lax.axis_index("fibre")
    r = lax.axis_index("rest")
    z = f // 2
    c = lax.rem(f, 2)
    other = z * 2 + (1 - c)

    barrier = pltpu.get_barrier_semaphore()
    for d in range(1, NF):
        pl.semaphore_signal(barrier, inc=1, device_id={"fibre": wrap(f + d, NF)}, device_id_type=pl.DeviceIdType.MESH)
    for d in range(1, NR):
        pl.semaphore_signal(barrier, inc=1, device_id={"rest": wrap(r + d, NR)}, device_id_type=pl.DeviceIdType.MESH)

    own_copy = pltpu.make_async_copy(slab.at[:, pl.ds(pl.multiple_of(f * OWN, OWN), OWN)], got.at[f], s_own)
    own_copy.start()
    pl.semaphore_wait(barrier, NF - 1 + NR - 1)

    def x_copy(ch, d):
        to = wrap(f + d, NF)
        return remote(
            slab.at[:, pl.ds(pl.multiple_of(to * OWN + ch * CW, CW), CW)],
            got.at[f, :, pl.ds(ch * CW, CW)],
            s_x.at[ch, d], r_x.at[ch, d], {"fibre": to},
        )

    for ch in range(CHUNKS):
        for d in range(1, NF):
            x_copy(ch, d).start()
    fc[pl.ds(I1, PAD1 - I1), :] = jnp.zeros((PAD1 - I1, OWN), F32)
    own_copy.wait()
    for ch in range(CHUNKS):
        for d in range(1, NF):
            x_copy(ch, d).wait_recv()
        cols = pl.ds(ch * CW, CW)
        for s in range(NF):
            fc[pl.ds(s * ROWS, ROWS), cols] = got[s, :, cols]
        hi, lo = split(fc[:, cols])
        for k in range(3):
            top, wide = k * 256, (k + 1) * 256
            new = dot3((hi[top:top + 256], lo[top:top + 256]), (hi[:wide], lo[:wide]), NT)
            if ch == 0:
                acc[pl.ds(top, 256), pl.ds(0, wide)] = new
            else:
                acc[pl.ds(top, 256), pl.ds(0, wide)] += new
    f_copy = pltpu.make_async_copy(fc.at[pl.ds(0, I1), :], f_out, s_o)
    f_copy.start()

    def put(b, value):
        part[b // 8, pl.ds((2 * b) % 16, 2)] = value.reshape(2, 8, 8, 128)

    def blk(i, j, rows=128):
        return acc[pl.ds(i * 128, rows), pl.ds(j * 128, 128)]

    row_id = lax.broadcasted_iota(jnp.int32, (128, 128), 0)
    col_id = lax.broadcasted_iota(jnp.int32, (128, 128), 1)
    for b, (i, j) in enumerate(OFF_DIAG):
        put(b, blk(i, j))
    second = blk(1, 1)
    put(10, jnp.where(row_id >= col_id, blk(0, 0), second))
    for k in range(2, 5):
        put(9 + k, blk(k, k))
    put(14, jnp.concatenate([blk(5, j, 32) for j in range(4)], axis=0))
    diagonal = jnp.sum(jnp.where(row_id == col_id, second, 0.0), axis=0, keepdims=True)
    put(15, jnp.concatenate(
        [blk(5, 4, 32), blk(5, 5, 32), jnp.broadcast_to(diagonal, (8, 128)), jnp.zeros((56, 128), F32)], axis=0))

    a_copy = remote(part.at[1 - c], ra, s_a, r_a, {"fibre": other})
    a_copy.start()
    a_copy.wait_recv()
    sa[...] = part[c] + ra[...]

    def b_copy(d):
        to = wrap(r + d, NR)
        return remote(sa.at[to], rb.at[d], s_b.at[d], r_b.at[d], {"rest": to})

    for d in range(1, NR):
        b_copy(d).start()
    total = sa[r]
    for d in range(1, NR):
        b_copy(d).wait_recv()
        total = total + rb[d]
    own[...] = total

    def c_copy(d):
        to = wrap(z + d, NZ)
        return remote(own.at[to], rc.at[d], s_c.at[d], r_c.at[d], {"fibre": to * 2 + c})

    for d in range(1, NZ):
        c_copy(d).start()
    tile = own[z]
    for d in range(1, NZ):
        c_copy(d).wait_recv()
        tile = tile + rc[d]
    mine[...] = tile
    full[c, r, z] = tile

    def d_copy(d):
        return remote(mine, full.at[c, r, z], s_d.at[d], r_d.at[d], {"fibre": wrap(z + d, NZ) * 2 + c})

    for d in range(1, NZ):
        d_copy(d).start()
    for d in range(1, NZ):
        d_copy(d).wait_recv()

    def e_copy(d):
        return remote(full.at[c, r], full.at[c, r], s_e.at[d], r_e.at[d], {"rest": wrap(r + d, NR)})

    def f_pass(d):
        at = wrap(r - d, NR)
        return remote(full.at[c, at], full.at[c, at], s_f.at[d], r_f.at[d], {"fibre": other})

    for d in range(1, NR):
        e_copy(d).start()
    f_pass(0).start()
    for d in range(1, NR):
        e_copy(d).wait_recv()
        f_pass(d).start()
    for d in range(NR):
        f_pass(d).wait_recv()
    g_copy = pltpu.make_async_copy(full, g_out, s_g)
    g_copy.start()

    for ch in range(CHUNKS):
        for d in range(1, NF):
            x_copy(ch, d).wait_send()
    a_copy.wait_send()
    for d in range(1, NR):
        b_copy(d).wait_send()
    for d in range(1, NZ):
        c_copy(d).wait_send()
        d_copy(d).wait_send()
    for d in range(1, NR):
        e_copy(d).wait_send()
    for d in range(NR):
        f_pass(d).wait_send()
    f_copy.wait()
    g_copy.wait()


def gram_call(slab):
    dma = pltpu.SemaphoreType.DMA
    any_spec = pl.BlockSpec(memory_space=pl.ANY)
    return pl.pallas_call(
        gram_kernel,
        out_shape=(
            jax.ShapeDtypeStruct((I1, OWN), F32),
            jax.ShapeDtypeStruct((2, NR, NZ, 8, 128), F32),
        ),
        in_specs=[any_spec],
        out_specs=(any_spec, any_spec),
        scratch_shapes=[
            pltpu.VMEM((NF, ROWS, OWN), F32),
            pltpu.VMEM((PAD1, OWN), F32),
            pltpu.VMEM((PAD1, PAD1), F32),
            pltpu.VMEM((2, NR, NZ, 8, 128), F32),
            pltpu.VMEM((NR, NZ, 8, 128), F32),
            pltpu.VMEM((NR, NZ, 8, 128), F32),
            pltpu.VMEM((NR, NZ, 8, 128), F32),
            pltpu.VMEM((NZ, 8, 128), F32),
            pltpu.VMEM((NZ, 8, 128), F32),
            pltpu.VMEM((8, 128), F32),
            pltpu.VMEM((2, NR, NZ, 8, 128), F32),
            dma,
            dma((CHUNKS, NF)), dma((CHUNKS, NF)),
            dma, dma,
            dma((NR,)), dma((NR,)),
            dma((NZ,)), dma((NZ,)),
            dma((NZ,)), dma((NZ,)),
            dma((NR,)), dma((NR,)),
            dma((NR,)), dma((NR,)),
            dma, dma,
        ],
        compiler_params=pltpu.CompilerParams(
            collective_id=0, has_side_effects=True, vmem_limit_bytes=VMEM_LIMIT),
        name="gram",
    )(slab)


def inverse_factor(small):
    count = RANK // 8
    tiles = [small[8 * t:8 * t + 8] for t in range(count)]
    lane = lax.broadcasted_iota(jnp.int32, (8, 128), 1)
    sub = lax.broadcasted_iota(jnp.int32, (8, 128), 0)

    def over_lanes(v, j):
        return jnp.broadcast_to(v[:, j:j + 1], (8, 128))

    def over_rows(v, k):
        return jnp.broadcast_to(v[k:k + 1, :], (8, 128))

    out = []
    for t in range(count):
        v = tiles[t]
        cols = [over_lanes(v, 8 * t + k) for k in range(8)]
        below = [[over_lanes(tiles[r], 8 * t + k) for k in range(8)] for r in range(t + 1, count)]
        kept = jnp.zeros((8, 128), F32)
        pivots = jnp.ones((8, 128), F32)
        for k in range(8):
            at = sub == k
            here = lane == 8 * t + k
            pivot = over_rows(cols[k], k)
            inv = 1.0 / pivot
            row = jnp.where(here, 1.0, over_rows(v, k))
            kept = jnp.where(at, row, kept)
            pivots = jnp.where(at, pivot, pivots)
            scaled = row * inv
            v = jnp.where(at, scaled, jnp.where(here, 0.0, v) - cols[k] * scaled)
            for m in range(k + 1, 8):
                entry = over_rows(cols[m], k) * inv
                cols[m] = jnp.where(at, entry, cols[m] - cols[k] * entry)
        rows = [over_rows(v, k) for k in range(8)]
        block = (lane >= 8 * t) & (lane < 8 * t + 8)
        for r in range(t + 1, count):
            p = [below[r - t - 1][k] * rows[k] for k in range(8)]
            total = ((p[0] + p[1]) + (p[2] + p[3])) + ((p[4] + p[5]) + (p[6] + p[7]))
            tiles[r] = jnp.where(block, 0.0, tiles[r]) - total
        out.append(jnp.where(lane <= sub + 8 * t, kept * lax.rsqrt(pivots), 0.0))
    return jnp.concatenate(out, axis=0)


def iterate_kernel(g, start, fibres, factor, core, gh, gl, basis, fh, fl):
    row_id = lax.broadcasted_iota(jnp.int32, (128, 128), 0)
    col_id = lax.broadcasted_iota(jnp.int32, (128, 128), 1)

    def get(b):
        return g[b // 8, pl.ds((2 * b) % 16, 2)].reshape(128, 128)

    def store(i, j, value):
        hi, lo = split(value)
        at = (pl.ds(i * 128, 128), pl.ds(j * 128, 128))
        gh[at] = hi
        gl[at] = lo

    for b, (i, j) in enumerate(OFF_DIAG):
        value = get(b)
        store(i, j, value)
        store(j, i, value.T)
    for k in range(2, 5):
        store(k, k, get(9 + k))
    last = get(15)
    both = get(10)
    flip = both.T
    store(0, 0, jnp.where(row_id >= col_id, both, flip))
    diagonal = jnp.broadcast_to(last[64:65], (128, 128))
    store(1, 1, jnp.where(row_id < col_id, both, jnp.where(row_id > col_id, flip, diagonal)))
    most = get(14)
    strips = [most[32 * k:32 * k + 32] for k in range(4)] + [last[0:32], last[32:64]]
    for j, strip in enumerate(strips):
        value = jnp.concatenate([strip, jnp.zeros((96, 128), F32)], axis=0)
        store(5, j, value)
        if j < 5:
            store(j, 5, value.T)

    fh[...], fl[...] = split(fibres[...])
    basis[...] = jnp.concatenate([start[...], jnp.zeros((RANK, PAD1 - I1), F32)], axis=1)

    def step(_, carry):
        image = dot3(split(basis[...]), (gh[...], gl[...]), NN)
        wide = jnp.concatenate([image, jnp.zeros((128 - RANK, PAD1), F32)], axis=0)
        small = lax.dot_general(image, wide, NT, precision=HP, preferred_element_type=F32)
        inverse = inverse_factor(small)[:, :RANK]
        basis[...] = lax.dot_general(inverse, image, NN, precision=HP, preferred_element_type=F32)
        return carry

    lax.fori_loop(0, ITERS, step, 0)
    last_basis = basis[...]
    factor[...] = last_basis[:, :I1]
    product = dot3(split(last_basis[:, :I1]), (fh[...], fl[...]), NN)
    for j in range(NF):
        core[j] = product[6 * j:6 * j + 6]


def iterate_call(g, start, fibres):
    vmem = pl.BlockSpec(memory_space=pltpu.VMEM)
    return pl.pallas_call(
        iterate_kernel,
        out_shape=(
            jax.ShapeDtypeStruct((RANK, I1), F32),
            jax.ShapeDtypeStruct((NF, RANK // NF, OWN), F32),
        ),
        in_specs=[vmem, vmem, vmem],
        out_specs=(vmem, vmem),
        scratch_shapes=[
            pltpu.VMEM((PAD1, PAD1), BF16),
            pltpu.VMEM((PAD1, PAD1), BF16),
            pltpu.VMEM((RANK, PAD1), F32),
            pltpu.VMEM((I1, OWN), BF16),
            pltpu.VMEM((I1, OWN), BF16),
        ],
        compiler_params=pltpu.CompilerParams(vmem_limit_bytes=VMEM_LIMIT),
        name="iterate",
    )(g, start, fibres)


def core_kernel(blocks, out, s_own, s_x, r_x):
    f = lax.axis_index("fibre")
    barrier = pltpu.get_barrier_semaphore()
    for d in range(1, NF):
        pl.semaphore_signal(barrier, inc=1, device_id={"fibre": wrap(f + d, NF)}, device_id_type=pl.DeviceIdType.MESH)
    at = pl.ds(pl.multiple_of(f * OWN, OWN), OWN)
    own_copy = pltpu.make_async_copy(blocks.at[f], out.at[:, at], s_own)
    own_copy.start()
    pl.semaphore_wait(barrier, NF - 1)

    def copy(d):
        to = wrap(f + d, NF)
        return remote(blocks.at[to], out.at[:, at], s_x.at[d], r_x.at[d], {"fibre": to})

    for d in range(1, NF):
        copy(d).start()
    own_copy.wait()
    for d in range(1, NF):
        copy(d).wait()


def core_call(blocks):
    dma = pltpu.SemaphoreType.DMA
    any_spec = pl.BlockSpec(memory_space=pl.ANY)
    return pl.pallas_call(
        core_kernel,
        out_shape=jax.ShapeDtypeStruct((RANK // NF, COLS), F32),
        in_specs=[any_spec],
        out_specs=any_spec,
        scratch_shapes=[dma, dma((NF,)), dma((NF,))],
        compiler_params=pltpu.CompilerParams(
            collective_id=1, has_side_effects=True, vmem_limit_bytes=VMEM_LIMIT),
        name="core",
    )(blocks)


def shards(slab, start_basis):
    fibres, gram = gram_call(slab)
    factor, blocks = iterate_call(gram, start_basis.T, fibres)
    return factor.T, core_call(blocks)


def solution(mesh):
    return jax.shard_map(
        shards,
        mesh=mesh,
        in_specs=(P("fibre", "rest"), P()),
        out_specs=(P(), P("fibre", "rest")),
        check_vma=False,
    )
```

```python
import jax
import jax.numpy as jnp
from jax import lax
from jax.experimental import pallas as pl
from jax.experimental.pallas import tpu as pltpu
from jax.sharding import PartitionSpec as P

ITERS = 3
HP = lax.Precision.HIGHEST
F32 = jnp.float32
BF16 = jnp.bfloat16
NF = 16
NR = 16
NZ = 8
ROWS = 42
I1 = 672
PAD1 = 768
RANK = 96
COLS = 16384
OWN = 1024
VMEM_LIMIT = 56 * 1024 * 1024

NT = (((1,), (1,)), ((), ()))
NN = (((1,), (0,)), ((), ()))


def split(x):
    hi = x.astype(BF16)
    lo = (x - hi.astype(F32)).astype(BF16)
    return hi, lo


def dot3(a, b, dims):
    ah, al = a
    bh, bl = b

    def d(u, v):
        return lax.dot_general(u, v, dims, preferred_element_type=F32)

    return d(ah, bh) + (d(ah, bl) + d(al, bh))


def remote(src, dst, send, recv, device):
    return pltpu.make_async_remote_copy(
        src_ref=src, dst_ref=dst, send_sem=send, recv_sem=recv,
        device_id=device, device_id_type=pl.DeviceIdType.MESH,
    )


def wrap(v, n):
    return lax.rem(v + n, n)


ROW_B, ROW_C, ROW_T = 256, 512, 640
EARLY = [(i, j) for i in range(4) for j in range(i + 1)]
LATE = [(4, j) for j in range(5)]
T3 = 3


def mesh_signal(sem, device):
    pl.semaphore_signal(sem, inc=1, device_id=device, device_id_type=pl.DeviceIdType.MESH)


def gram_kernel(slab, f_out, g_out, g2_out, fc, fh, fl, tail, tail_out, tail_in,
                part, ra, sa, rb, own, rc, mine, full, part2, ra2, sa2, rb2, own2, rz2, full2,
                s_own, s_x, r_x, s_a, r_a, s_b, r_b, s_c, r_c, s_d, r_d, s_e, r_e, s_f, r_f,
                s_a2, r_a2, s_b2, r_b2, s_c2, r_c2, s_e2, r_e2, s_f2, r_f2, s_o, s_g):
    f = lax.axis_index("fibre")
    r = lax.axis_index("rest")
    z = f // 2
    c = lax.rem(f, 2)
    other = z * 2 + (1 - c)

    barrier = pltpu.get_barrier_semaphore()
    for d in range(1, NF):
        mesh_signal(barrier, {"fibre": wrap(f + d, NF)})
    for d in range(1, NR):
        mesh_signal(barrier, {"rest": wrap(r + d, NR)})

    sets = [(0, 16, 0), (16, 16, ROW_B), (32, 8, ROW_C)]

    def piece(k, to):
        at, rows, _ = sets[k]
        return slab.at[pl.ds(at, rows), pl.ds(pl.multiple_of(to * OWN, OWN), OWN)]

    def place(k):
        _, rows, base = sets[k]
        return fc.at[pl.ds(pl.multiple_of(base + f * rows, rows), rows), :]

    def x_copy(k, d):
        to = wrap(f + d, NF)
        return remote(piece(k, to), place(k), s_x.at[k, d], r_x.at[k, d], {"fibre": to})

    def t_copy(d):
        to = wrap(f + d, NF)
        return remote(tail_out.at[to], tail_in.at[f], s_x.at[3, d], r_x.at[3, d], {"fibre": to})

    tail_copy = pltpu.make_async_copy(slab.at[pl.ds(40, 2), :], tail.at[pl.ds(0, 2), :], s_own.at[3])
    tail_copy.start()
    own_copies = [pltpu.make_async_copy(piece(k, f), place(k), s_own.at[k]) for k in range(3)]
    for copy in own_copies:
        copy.start()
    pl.semaphore_wait(barrier, NF - 1 + NR - 1)

    for d in range(1, NF):
        x_copy(0, d).start()
    tail_copy.wait()
    for to in range(NF):
        for k in range(8):
            both = tail[0:2, pl.ds((to * 8 + k) * 128, 128)]
            tail_out[to, 0, k:k + 1, :] = both[0:1]
            tail_out[to, 1, k:k + 1, :] = both[1:2]
    tail_in[f] = tail_out[f]
    for d in range(1, NF):
        t_copy(d).start()
    for k in (1, 2):
        for d in range(1, NF):
            x_copy(k, d).start()

    def rounded(top, rows):
        at = pl.ds(top, rows)
        fh[at, :], fl[at, :] = split(fc[at, :])

    def pair(top, rows):
        return fh[pl.ds(top, rows), :], fl[pl.ds(top, rows), :]

    def put(b, value):
        part[b // 8, pl.ds((2 * b) % 16, 2)] = value.reshape(2, 8, 8, 128)

    def put2(tile, value):
        for k in range(value.shape[0] // 8):
            n = tile + k
            part2[n // (NR * T3), (n // T3) % NR, n % T3] = value[8 * k:8 * k + 8]

    fc[pl.ds(I1, PAD1 - I1), :] = jnp.zeros((PAD1 - I1, OWN), F32)
    own_copies[0].wait()
    for d in range(1, NF):
        x_copy(0, d).wait_recv()
    rounded(0, 256)
    block = dot3(pair(0, 256), pair(0, 256), NT)
    for b in range(3):
        i, j = EARLY[b]
        put(b, block[128 * i:128 * i + 128, 128 * j:128 * j + 128])

    for d in range(1, NF):
        t_copy(d).wait_recv()
    for i in range(2):
        for k in range(8):
            fc[pl.ds(ROW_T + 16 * i, 16), pl.ds(128 * k, 128)] = jnp.concatenate(
                [tail_in[s, i, k:k + 1, :] for s in range(NF)], axis=0)
    rounded(ROW_T, PAD1 - ROW_T)
    own_copies[1].wait()
    for d in range(1, NF):
        x_copy(1, d).wait_recv()
    rounded(ROW_B, 256)
    block = dot3(pair(ROW_B, 256), pair(0, 512), NT)
    for b in range(3, 10):
        i, j = EARLY[b]
        put(b, block[128 * (i - 2):128 * (i - 2) + 128, 128 * j:128 * j + 128])
    strip = dot3(pair(ROW_T, 32), pair(0, 512), NT)
    put(10, jnp.concatenate([strip[:, 128 * j:128 * j + 128] for j in range(4)], axis=0))
    corner = dot3(pair(ROW_T, 32), pair(ROW_T, 128), NT)
    put(11, jnp.concatenate([corner, jnp.zeros((96, 128), F32)], axis=0))
    for b in range(12, 16):
        put(b, jnp.zeros((128, 128), F32))

    a_copy = remote(part.at[1 - c], ra, s_a, r_a, {"fibre": other})
    a_copy.start()
    a_copy.wait_recv()
    sa[...] = part[c] + ra[...]

    def b_copy(d):
        to = wrap(r + d, NR)
        return remote(sa.at[to], rb.at[d], s_b.at[d], r_b.at[d], {"rest": to})

    for d in range(1, NR):
        b_copy(d).start()
    total = sa[r]
    for d in range(1, NR):
        b_copy(d).wait_recv()
        total = total + rb[d]
    own[...] = total

    def c_copy(d):
        to = wrap(z + d, NZ)
        return remote(own.at[to], rc.at[d], s_c.at[d], r_c.at[d], {"fibre": to * 2 + c})

    for d in range(1, NZ):
        c_copy(d).start()

    own_copies[2].wait()
    for d in range(1, NF):
        x_copy(2, d).wait_recv()
    rounded(ROW_C, 128)
    block = dot3(pair(ROW_C, 128), pair(0, 640), NT)
    for j in range(5):
        put2(16 * j, block[:, 128 * j:128 * j + 128])
    put2(80, dot3(pair(ROW_T, 32), pair(ROW_C, 128), NT))
    put2(84, jnp.zeros((96, 128), F32))
    a2_copy = remote(part2.at[1 - c], ra2, s_a2, r_a2, {"fibre": other})
    a2_copy.start()
    f_copy = pltpu.make_async_copy(fc.at[pl.ds(0, I1), :], f_out, s_o)
    f_copy.start()

    tile = own[z]
    for d in range(1, NZ):
        c_copy(d).wait_recv()
        tile = tile + rc[d]
    mine[...] = tile
    full[c, r, z] = tile

    def d_copy(d):
        return remote(mine, full.at[c, r, z], s_d.at[d], r_d.at[d], {"fibre": wrap(z + d, NZ) * 2 + c})

    for d in range(1, NZ):
        d_copy(d).start()

    a2_copy.wait_recv()
    sa2[...] = part2[c] + ra2[...]

    def b2_copy(d):
        to = wrap(r + d, NR)
        return remote(sa2.at[to], rb2.at[d], s_b2.at[d], r_b2.at[d], {"rest": to})

    for d in range(1, NR):
        b2_copy(d).start()

    def e_copy(d):
        return remote(full.at[c, r], full.at[c, r], s_e.at[d], r_e.at[d], {"rest": wrap(r + d, NR)})

    def f_pass(d):
        at = wrap(r - d, NR)
        return remote(full.at[c, at], full.at[c, at], s_f.at[d], r_f.at[d], {"fibre": other})

    for d in range(1, NZ):
        d_copy(d).wait_recv()
    for d in range(1, NR):
        e_copy(d).start()
    f_pass(0).start()

    total2 = sa2[r]
    for d in range(1, NR):
        b2_copy(d).wait_recv()
        total2 = total2 + rb2[d]
    own2[...] = total2
    rz2[z] = total2

    def c2_copy(d):
        return remote(own2, rz2.at[z], s_c2.at[d], r_c2.at[d], {"fibre": wrap(z + d, NZ) * 2 + c})

    for d in range(1, NZ):
        c2_copy(d).start()
    for d in range(1, NZ):
        c2_copy(d).wait_recv()
    full2[c, r] = ((rz2[0] + rz2[1]) + (rz2[2] + rz2[3])) + ((rz2[4] + rz2[5]) + (rz2[6] + rz2[7]))

    def e2_copy(d):
        return remote(full2.at[c, r], full2.at[c, r], s_e2.at[d], r_e2.at[d], {"rest": wrap(r + d, NR)})

    def f2_pass(d):
        at = wrap(r - d, NR)
        return remote(full2.at[c, at], full2.at[c, at], s_f2.at[d], r_f2.at[d], {"fibre": other})

    for d in range(1, NR):
        e2_copy(d).start()
    f2_pass(0).start()

    for d in range(1, NR):
        e_copy(d).wait_recv()
        f_pass(d).start()
    for d in range(1, NR):
        e2_copy(d).wait_recv()
        f2_pass(d).start()
    for d in range(NR):
        f_pass(d).wait_recv()
    g_copy = pltpu.make_async_copy(full, g_out, s_g.at[0])
    g_copy.start()
    for d in range(NR):
        f2_pass(d).wait_recv()
    g2_copy = pltpu.make_async_copy(full2, g2_out, s_g.at[1])
    g2_copy.start()

    for d in range(1, NF):
        t_copy(d).wait_send()
        for k in range(3):
            x_copy(k, d).wait_send()
    a_copy.wait_send()
    a2_copy.wait_send()
    for d in range(1, NZ):
        c_copy(d).wait_send()
        d_copy(d).wait_send()
        c2_copy(d).wait_send()
    for d in range(1, NR):
        b_copy(d).wait_send()
        b2_copy(d).wait_send()
        e_copy(d).wait_send()
        e2_copy(d).wait_send()
    for d in range(NR):
        f_pass(d).wait_send()
        f2_pass(d).wait_send()
    f_copy.wait()
    g_copy.wait()
    g2_copy.wait()


def gram_call(slab):
    dma = pltpu.SemaphoreType.DMA
    any_spec = pl.BlockSpec(memory_space=pl.ANY)

    def tiles(*shape):
        return pltpu.VMEM((*shape, 8, 128), F32)

    return pl.pallas_call(
        gram_kernel,
        out_shape=(
            jax.ShapeDtypeStruct((I1, OWN), F32),
            jax.ShapeDtypeStruct((2, NR, NZ, 8, 128), F32),
            jax.ShapeDtypeStruct((2, NR, T3, 8, 128), F32),
        ),
        in_specs=[any_spec],
        out_specs=(any_spec, any_spec, any_spec),
        scratch_shapes=[
            pltpu.VMEM((PAD1, OWN), F32),
            pltpu.VMEM((PAD1, OWN), BF16),
            pltpu.VMEM((PAD1, OWN), BF16),
            pltpu.VMEM((8, COLS), F32),
            tiles(NF, 2), tiles(NF, 2),
            tiles(2, NR, NZ), tiles(NR, NZ), tiles(NR, NZ), tiles(NR, NZ),
            tiles(NZ), tiles(NZ), tiles(), tiles(2, NR, NZ),
            tiles(2, NR, T3), tiles(NR, T3), tiles(NR, T3), tiles(NR, T3),
            tiles(T3), tiles(NZ, T3), tiles(2, NR, T3),
            dma((4,)),
            dma((4, NF)), dma((4, NF)),
            dma, dma,
            dma((NR,)), dma((NR,)),
            dma((NZ,)), dma((NZ,)),
            dma((NZ,)), dma((NZ,)),
            dma((NR,)), dma((NR,)),
            dma((NR,)), dma((NR,)),
            dma, dma,
            dma((NR,)), dma((NR,)),
            dma((NZ,)), dma((NZ,)),
            dma((NR,)), dma((NR,)),
            dma((NR,)), dma((NR,)),
            dma, dma((2,)),
        ],
        compiler_params=pltpu.CompilerParams(
            collective_id=0, has_side_effects=True, vmem_limit_bytes=VMEM_LIMIT),
        name="gram",
    )(slab)


def inverse_factor(small):
    count = RANK // 8
    tiles = [small[8 * t:8 * t + 8] for t in range(count)]
    lane = lax.broadcasted_iota(jnp.int32, (8, 128), 1)
    sub = lax.broadcasted_iota(jnp.int32, (8, 128), 0)

    def over_lanes(v, j):
        return jnp.broadcast_to(v[:, j:j + 1], (8, 128))

    def over_rows(v, k):
        return jnp.broadcast_to(v[k:k + 1, :], (8, 128))

    out = []
    for t in range(count):
        v = tiles[t]
        cols = [over_lanes(v, 8 * t + k) for k in range(8)]
        below = [[over_lanes(tiles[r], 8 * t + k) for k in range(8)] for r in range(t + 1, count)]
        kept = jnp.zeros((8, 128), F32)
        pivots = jnp.ones((8, 128), F32)
        for k in range(8):
            at = sub == k
            here = lane == 8 * t + k
            pivot = over_rows(cols[k], k)
            inv = 1.0 / pivot
            row = jnp.where(here, 1.0, over_rows(v, k))
            kept = jnp.where(at, row, kept)
            pivots = jnp.where(at, pivot, pivots)
            scaled = row * inv
            v = jnp.where(at, scaled, jnp.where(here, 0.0, v) - cols[k] * scaled)
            for m in range(k + 1, 8):
                entry = over_rows(cols[m], k) * inv
                cols[m] = jnp.where(at, entry, cols[m] - cols[k] * entry)
        rows = [over_rows(v, k) for k in range(8)]
        block = (lane >= 8 * t) & (lane < 8 * t + 8)
        for r in range(t + 1, count):
            p = [below[r - t - 1][k] * rows[k] for k in range(8)]
            total = ((p[0] + p[1]) + (p[2] + p[3])) + ((p[4] + p[5]) + (p[6] + p[7]))
            tiles[r] = jnp.where(block, 0.0, tiles[r]) - total
        out.append(jnp.where(lane <= sub + 8 * t, kept * lax.rsqrt(pivots), 0.0))
    return jnp.concatenate(out, axis=0)


def permutation(transposed):
    p = lax.broadcasted_iota(jnp.int32, (PAD1, PAD1), 0 if transposed else 1)
    i = lax.broadcasted_iota(jnp.int32, (PAD1, PAD1), 1 if transposed else 0)
    q = p - ROW_T
    wide = ROWS * ((p & 255) >> 4) + (p & 15) + jnp.where(p >= ROW_B, 16, 0)
    narrow = ROWS * ((p - ROW_C) >> 3) + 32 + (p & 7)
    rest = ROWS * (q & 15) + 40 + (q >> 4)
    row = jnp.where(p < ROW_C, wide, jnp.where(p < ROW_T, narrow, jnp.where(p < I1, rest, p)))
    return jnp.where(row == i, 1.0, 0.0).astype(BF16)


def permuted(x, ones):
    hi = x.astype(BF16)
    left = x - hi.astype(F32)
    mid = left.astype(BF16)
    low = (left - mid.astype(F32)).astype(BF16)

    def d(u):
        return lax.dot_general(u, ones, NN, preferred_element_type=F32)

    return d(hi) + (d(mid) + d(low))


def iterate_kernel(g, g2, start, fibres, factor, core, gh, gl, basis, fh, fl):
    def get(b):
        return g[b // 8, pl.ds((2 * b) % 16, 2)].reshape(128, 128)

    def get2(tile, count):
        at = range(tile, tile + count)
        return jnp.concatenate([g2[n // (NR * T3), (n // T3) % NR, n % T3] for n in at], axis=0)

    def store(i, j, value):
        hi, lo = split(value)
        at = (pl.ds(i * 128, 128), pl.ds(j * 128, 128))
        gh[at] = hi
        gl[at] = lo

    def store_both(i, j, value):
        store(i, j, value)
        if i != j:
            store(j, i, value.T)

    def deep(strip):
        return jnp.concatenate([strip, jnp.zeros((96, 128), F32)], axis=0)

    for b, (i, j) in enumerate(EARLY):
        store_both(i, j, get(b))
    strips = get(10)
    for j in range(4):
        store_both(5, j, deep(strips[32 * j:32 * j + 32]))
    store(5, 5, get(11))
    for j in range(5):
        store_both(4, j, get2(16 * j, 16))
    store_both(5, 4, deep(get2(80, 4)))

    fh[...], fl[...] = split(fibres[...])
    wide_start = jnp.concatenate([start[...], jnp.zeros((RANK, PAD1 - I1), F32)], axis=1)
    basis[...] = permuted(wide_start, permutation(False))

    def step(_, carry):
        image = dot3(split(basis[...]), (gh[...], gl[...]), NN)
        wide = jnp.concatenate([image, jnp.zeros((128 - RANK, PAD1), F32)], axis=0)
        small = lax.dot_general(image, wide, NT, precision=HP, preferred_element_type=F32)
        inverse = inverse_factor(small)[:, :RANK]
        basis[...] = lax.dot_general(inverse, image, NN, precision=HP, preferred_element_type=F32)
        return carry

    lax.fori_loop(0, ITERS, step, 0)
    last_basis = basis[...]
    factor[...] = permuted(last_basis, permutation(True))[:, :I1]
    product = dot3(split(last_basis[:, :I1]), (fh[...], fl[...]), NN)
    for j in range(NF):
        core[j] = product[6 * j:6 * j + 6]


def iterate_call(g, g2, start, fibres):
    vmem = pl.BlockSpec(memory_space=pltpu.VMEM)
    return pl.pallas_call(
        iterate_kernel,
        out_shape=(
            jax.ShapeDtypeStruct((RANK, I1), F32),
            jax.ShapeDtypeStruct((NF, RANK // NF, OWN), F32),
        ),
        in_specs=[vmem, vmem, vmem, vmem],
        out_specs=(vmem, vmem),
        scratch_shapes=[
            pltpu.VMEM((PAD1, PAD1), BF16),
            pltpu.VMEM((PAD1, PAD1), BF16),
            pltpu.VMEM((RANK, PAD1), F32),
            pltpu.VMEM((I1, OWN), BF16),
            pltpu.VMEM((I1, OWN), BF16),
        ],
        compiler_params=pltpu.CompilerParams(vmem_limit_bytes=VMEM_LIMIT),
        name="iterate",
    )(g, g2, start, fibres)


def core_kernel(blocks, out, s_own, s_x, r_x):
    f = lax.axis_index("fibre")
    barrier = pltpu.get_barrier_semaphore()
    for d in range(1, NF):
        pl.semaphore_signal(barrier, inc=1, device_id={"fibre": wrap(f + d, NF)}, device_id_type=pl.DeviceIdType.MESH)
    at = pl.ds(pl.multiple_of(f * OWN, OWN), OWN)
    own_copy = pltpu.make_async_copy(blocks.at[f], out.at[:, at], s_own)
    own_copy.start()
    pl.semaphore_wait(barrier, NF - 1)

    def copy(d):
        to = wrap(f + d, NF)
        return remote(blocks.at[to], out.at[:, at], s_x.at[d], r_x.at[d], {"fibre": to})

    for d in range(1, NF):
        copy(d).start()
    own_copy.wait()
    for d in range(1, NF):
        copy(d).wait()


def core_call(blocks):
    dma = pltpu.SemaphoreType.DMA
    any_spec = pl.BlockSpec(memory_space=pl.ANY)
    return pl.pallas_call(
        core_kernel,
        out_shape=jax.ShapeDtypeStruct((RANK // NF, COLS), F32),
        in_specs=[any_spec],
        out_specs=any_spec,
        scratch_shapes=[dma, dma((NF,)), dma((NF,))],
        compiler_params=pltpu.CompilerParams(
            collective_id=1, has_side_effects=True, vmem_limit_bytes=VMEM_LIMIT),
        name="core",
    )(blocks)


def shards(slab, start_basis):
    fibres, gram, gram2 = gram_call(slab)
    factor, blocks = iterate_call(gram, gram2, start_basis.T, fibres)
    return factor.T, core_call(blocks)


def solution(mesh):
    return jax.shard_map(
        shards,
        mesh=mesh,
        in_specs=(P("fibre", "rest"), P()),
        out_specs=(P(), P("fibre", "rest")),
        check_vma=False,
    )
```

```python
import jax
import jax.numpy as jnp
from jax import lax
from jax.experimental import pallas as pl
from jax.experimental.pallas import tpu as pltpu
from jax.sharding import PartitionSpec as P

ITERS = 3
HP = lax.Precision.HIGHEST
F32 = jnp.float32
BF16 = jnp.bfloat16
NF = 16
NR = 16
NZ = 8
ROWS = 42
I1 = 672
PAD1 = 768
RANK = 96
COLS = 16384
OWN = 1024
VMEM_LIMIT = 56 * 1024 * 1024

NT = (((1,), (1,)), ((), ()))
NN = (((1,), (0,)), ((), ()))


def split(x):
    hi = x.astype(BF16)
    lo = (x - hi.astype(F32)).astype(BF16)
    return hi, lo


def dot3(a, b, dims):
    ah, al = a
    bh, bl = b

    def d(u, v):
        return lax.dot_general(u, v, dims, preferred_element_type=F32)

    return d(ah, bh) + (d(ah, bl) + d(al, bh))


def remote(src, dst, send, recv, device):
    return pltpu.make_async_remote_copy(
        src_ref=src, dst_ref=dst, send_sem=send, recv_sem=recv,
        device_id=device, device_id_type=pl.DeviceIdType.MESH,
    )


def wrap(v, n):
    return lax.rem(v + n, n)


def inverse_factor(small):
    count = RANK // 8
    tiles = [small[8 * t:8 * t + 8] for t in range(count)]
    lane = lax.broadcasted_iota(jnp.int32, (8, 128), 1)
    sub = lax.broadcasted_iota(jnp.int32, (8, 128), 0)

    def over_lanes(v, j):
        return jnp.broadcast_to(v[:, j:j + 1], (8, 128))

    def over_rows(v, k):
        return jnp.broadcast_to(v[k:k + 1, :], (8, 128))

    out = []
    for t in range(count):
        v = tiles[t]
        cols = [over_lanes(v, 8 * t + k) for k in range(8)]
        below = [[over_lanes(tiles[r], 8 * t + k) for k in range(8)] for r in range(t + 1, count)]
        kept = jnp.zeros((8, 128), F32)
        pivots = jnp.ones((8, 128), F32)
        for k in range(8):
            at = sub == k
            here = lane == 8 * t + k
            pivot = over_rows(cols[k], k)
            inv = 1.0 / pivot
            row = jnp.where(here, 1.0, over_rows(v, k))
            kept = jnp.where(at, row, kept)
            pivots = jnp.where(at, pivot, pivots)
            scaled = row * inv
            v = jnp.where(at, scaled, jnp.where(here, 0.0, v) - cols[k] * scaled)
            for m in range(k + 1, 8):
                entry = over_rows(cols[m], k) * inv
                cols[m] = jnp.where(at, entry, cols[m] - cols[k] * entry)
        rows = [over_rows(v, k) for k in range(8)]
        block = (lane >= 8 * t) & (lane < 8 * t + 8)
        for r in range(t + 1, count):
            p = [below[r - t - 1][k] * rows[k] for k in range(8)]
            total = ((p[0] + p[1]) + (p[2] + p[3])) + ((p[4] + p[5]) + (p[6] + p[7]))
            tiles[r] = jnp.where(block, 0.0, tiles[r]) - total
        out.append(jnp.where(lane <= sub + 8 * t, kept * lax.rsqrt(pivots), 0.0))
    return jnp.concatenate(out, axis=0)


def permutation(transposed):
    p = lax.broadcasted_iota(jnp.int32, (PAD1, PAD1), 0 if transposed else 1)
    i = lax.broadcasted_iota(jnp.int32, (PAD1, PAD1), 1 if transposed else 0)
    q = p - ROW_T
    wide = ROWS * ((p & 255) >> 4) + (p & 15) + jnp.where(p >= ROW_B, 16, 0)
    narrow = ROWS * ((p - ROW_C) >> 3) + 32 + (p & 7)
    rest = ROWS * (q & 15) + 40 + (q >> 4)
    row = jnp.where(p < ROW_C, wide, jnp.where(p < ROW_T, narrow, jnp.where(p < I1, rest, p)))
    return jnp.where(row == i, 1.0, 0.0).astype(BF16)


def permuted(x, ones):
    hi = x.astype(BF16)
    left = x - hi.astype(F32)
    mid = left.astype(BF16)
    low = (left - mid.astype(F32)).astype(BF16)

    def d(u):
        return lax.dot_general(u, ones, NN, preferred_element_type=F32)

    return d(hi) + (d(mid) + d(low))


ROW_B, ROW_C, ROW_T = 256, 512, 640
EARLY = [(i, j) for i in range(4) for j in range(i + 1)]
LATE = [(4, j) for j in range(5)]
T3 = 3


def mesh_signal(sem, device):
    pl.semaphore_signal(sem, inc=1, device_id=device, device_id_type=pl.DeviceIdType.MESH)


def main_kernel(slab, start, factor, core, fc, fh, fl, tail, tail_out, tail_in, gh, gl, basis, turned, core_tiles,
                part, ra, sa, rb, own, rc, mine, full, part2, ra2, sa2, rb2, own2, rz2, full2,
                s_own, s_x, r_x, s_a, r_a, s_b, r_b, s_c, r_c, s_d, r_d, s_e, r_e, s_f, r_f,
                s_a2, r_a2, s_b2, r_b2, s_c2, r_c2, s_e2, r_e2, s_f2, r_f2, s_z, r_z, s_o):
    f = lax.axis_index("fibre")
    r = lax.axis_index("rest")
    z = f // 2
    c = lax.rem(f, 2)
    other = z * 2 + (1 - c)

    barrier = pltpu.get_barrier_semaphore()
    for d in range(1, NF):
        mesh_signal(barrier, {"fibre": wrap(f + d, NF)})
    for d in range(1, NR):
        mesh_signal(barrier, {"rest": wrap(r + d, NR)})

    sets = [(0, 16, 0), (16, 16, ROW_B), (32, 8, ROW_C)]

    def piece(k, to):
        at, rows, _ = sets[k]
        return slab.at[pl.ds(at, rows), pl.ds(pl.multiple_of(to * OWN, OWN), OWN)]

    def place(k):
        _, rows, base = sets[k]
        return fc.at[pl.ds(pl.multiple_of(base + f * rows, rows), rows), :]

    def x_copy(k, d):
        to = wrap(f + d, NF)
        return remote(piece(k, to), place(k), s_x.at[k, d], r_x.at[k, d], {"fibre": to})

    def t_copy(d):
        to = wrap(f + d, NF)
        return remote(tail_out.at[to], tail_in.at[f], s_x.at[3, d], r_x.at[3, d], {"fibre": to})

    tail_copy = pltpu.make_async_copy(slab.at[pl.ds(40, 2), :], tail.at[pl.ds(0, 2), :], s_own.at[3])
    tail_copy.start()
    own_copies = [pltpu.make_async_copy(piece(k, f), place(k), s_own.at[k]) for k in range(3)]
    for copy in own_copies:
        copy.start()
    pl.semaphore_wait(barrier, NF - 1 + NR - 1)

    for d in range(1, NF):
        x_copy(0, d).start()
    tail_copy.wait()
    for to in range(NF):
        for k in range(8):
            both = tail[0:2, pl.ds((to * 8 + k) * 128, 128)]
            tail_out[to, 0, k:k + 1, :] = both[0:1]
            tail_out[to, 1, k:k + 1, :] = both[1:2]
    tail_in[f] = tail_out[f]
    for d in range(1, NF):
        t_copy(d).start()
    for k in (1, 2):
        for d in range(1, NF):
            x_copy(k, d).start()

    def rounded(top, rows):
        at = pl.ds(top, rows)
        fh[at, :], fl[at, :] = split(fc[at, :])

    def pair(top, rows):
        return fh[pl.ds(top, rows), :], fl[pl.ds(top, rows), :]

    def put(b, value):
        part[b // 8, pl.ds((2 * b) % 16, 2)] = value.reshape(2, 8, 8, 128)

    def put2(tile, value):
        for k in range(value.shape[0] // 8):
            n = tile + k
            part2[n // (NR * T3), (n // T3) % NR, n % T3] = value[8 * k:8 * k + 8]

    fc[pl.ds(I1, PAD1 - I1), :] = jnp.zeros((PAD1 - I1, OWN), F32)
    wide_start = jnp.concatenate([start[...], jnp.zeros((RANK, PAD1 - I1), F32)], axis=1)
    basis[...] = permuted(wide_start, permutation(False))
    own_copies[0].wait()
    for d in range(1, NF):
        x_copy(0, d).wait_recv()
    rounded(0, 256)
    block = dot3(pair(0, 256), pair(0, 256), NT)
    for b in range(3):
        i, j = EARLY[b]
        put(b, block[128 * i:128 * i + 128, 128 * j:128 * j + 128])

    for d in range(1, NF):
        t_copy(d).wait_recv()
    for i in range(2):
        for k in range(8):
            fc[pl.ds(ROW_T + 16 * i, 16), pl.ds(128 * k, 128)] = jnp.concatenate(
                [tail_in[s, i, k:k + 1, :] for s in range(NF)], axis=0)
    rounded(ROW_T, PAD1 - ROW_T)
    own_copies[1].wait()
    for d in range(1, NF):
        x_copy(1, d).wait_recv()
    rounded(ROW_B, 256)
    block = dot3(pair(ROW_B, 256), pair(0, 512), NT)
    for b in range(3, 10):
        i, j = EARLY[b]
        put(b, block[128 * (i - 2):128 * (i - 2) + 128, 128 * j:128 * j + 128])
    strip = dot3(pair(ROW_T, 32), pair(0, 512), NT)
    put(10, jnp.concatenate([strip[:, 128 * j:128 * j + 128] for j in range(4)], axis=0))
    corner = dot3(pair(ROW_T, 32), pair(ROW_T, 128), NT)
    put(11, jnp.concatenate([corner, jnp.zeros((96, 128), F32)], axis=0))
    for b in range(12, 16):
        put(b, jnp.zeros((128, 128), F32))

    a_copy = remote(part.at[1 - c], ra, s_a, r_a, {"fibre": other})
    a_copy.start()
    a_copy.wait_recv()
    sa[...] = part[c] + ra[...]

    def b_copy(d):
        to = wrap(r + d, NR)
        return remote(sa.at[to], rb.at[d], s_b.at[d], r_b.at[d], {"rest": to})

    for d in range(1, NR):
        b_copy(d).start()
    total = sa[r]
    for d in range(1, NR):
        b_copy(d).wait_recv()
        total = total + rb[d]
    own[...] = total

    def c_copy(d):
        to = wrap(z + d, NZ)
        return remote(own.at[to], rc.at[d], s_c.at[d], r_c.at[d], {"fibre": to * 2 + c})

    for d in range(1, NZ):
        c_copy(d).start()

    own_copies[2].wait()
    for d in range(1, NF):
        x_copy(2, d).wait_recv()
    rounded(ROW_C, 128)
    block = dot3(pair(ROW_C, 128), pair(0, 640), NT)
    for j in range(5):
        put2(16 * j, block[:, 128 * j:128 * j + 128])
    put2(80, dot3(pair(ROW_T, 32), pair(ROW_C, 128), NT))
    put2(84, jnp.zeros((96, 128), F32))
    a2_copy = remote(part2.at[1 - c], ra2, s_a2, r_a2, {"fibre": other})
    a2_copy.start()

    tile = own[z]
    for d in range(1, NZ):
        c_copy(d).wait_recv()
        tile = tile + rc[d]
    mine[...] = tile
    full[c, r, z] = tile

    def d_copy(d):
        return remote(mine, full.at[c, r, z], s_d.at[d], r_d.at[d], {"fibre": wrap(z + d, NZ) * 2 + c})

    for d in range(1, NZ):
        d_copy(d).start()

    a2_copy.wait_recv()
    sa2[...] = part2[c] + ra2[...]

    def b2_copy(d):
        to = wrap(r + d, NR)
        return remote(sa2.at[to], rb2.at[d], s_b2.at[d], r_b2.at[d], {"rest": to})

    for d in range(1, NR):
        b2_copy(d).start()

    def e_copy(d):
        return remote(full.at[c, r], full.at[c, r], s_e.at[d], r_e.at[d], {"rest": wrap(r + d, NR)})

    def f_pass(d):
        at = wrap(r - d, NR)
        return remote(full.at[c, at], full.at[c, at], s_f.at[d], r_f.at[d], {"fibre": other})

    for d in range(1, NZ):
        d_copy(d).wait_recv()
    for d in range(1, NR):
        e_copy(d).start()
    f_pass(0).start()

    total2 = sa2[r]
    for d in range(1, NR):
        b2_copy(d).wait_recv()
        total2 = total2 + rb2[d]
    own2[...] = total2
    rz2[z] = total2

    def c2_copy(d):
        return remote(own2, rz2.at[z], s_c2.at[d], r_c2.at[d], {"fibre": wrap(z + d, NZ) * 2 + c})

    for d in range(1, NZ):
        c2_copy(d).start()
    for d in range(1, NZ):
        c2_copy(d).wait_recv()
    full2[c, r] = ((rz2[0] + rz2[1]) + (rz2[2] + rz2[3])) + ((rz2[4] + rz2[5]) + (rz2[6] + rz2[7]))

    def e2_copy(d):
        return remote(full2.at[c, r], full2.at[c, r], s_e2.at[d], r_e2.at[d], {"rest": wrap(r + d, NR)})

    def f2_pass(d):
        at = wrap(r - d, NR)
        return remote(full2.at[c, at], full2.at[c, at], s_f2.at[d], r_f2.at[d], {"fibre": other})

    for d in range(1, NR):
        e2_copy(d).start()
    f2_pass(0).start()

    for d in range(1, NR):
        e_copy(d).wait_recv()
        f_pass(d).start()
    for d in range(NR):
        f_pass(d).wait_recv()

    def store(i, j, value):
        hi, lo = split(value)
        at = (pl.ds(i * 128, 128), pl.ds(j * 128, 128))
        gh[at] = hi
        gl[at] = lo

    def store_both(i, j, value):
        store(i, j, value)
        if i != j:
            store(j, i, value.T)

    def get(b):
        return full[b // 8, pl.ds((2 * b) % 16, 2)].reshape(128, 128)

    def get2(tile, count):
        at = range(tile, tile + count)
        return jnp.concatenate([full2[n // (NR * T3), (n // T3) % NR, n % T3] for n in at], axis=0)

    def deep(value):
        return jnp.concatenate([value, jnp.zeros((96, 128), F32)], axis=0)

    for b, (i, j) in enumerate(EARLY):
        store_both(i, j, get(b))
    strips = get(10)
    for j in range(4):
        store_both(5, j, deep(strips[32 * j:32 * j + 32]))
    store(5, 5, get(11))

    for d in range(1, NR):
        e2_copy(d).wait_recv()
        f2_pass(d).start()
    for d in range(NR):
        f2_pass(d).wait_recv()
    for j in range(5):
        store_both(4, j, get2(16 * j, 16))
    store_both(5, 4, deep(get2(80, 4)))

    def step(_, carry):
        image = dot3(split(basis[...]), (gh[...], gl[...]), NN)
        wide = jnp.concatenate([image, jnp.zeros((128 - RANK, PAD1), F32)], axis=0)
        small = lax.dot_general(image, wide, NT, precision=HP, preferred_element_type=F32)
        inverse = inverse_factor(small)[:, :RANK]
        basis[...] = lax.dot_general(inverse, image, NN, precision=HP, preferred_element_type=F32)
        return carry

    lax.fori_loop(0, ITERS, step, 0)

    product = dot3(split(basis[...]), (fh[...], fl[...]), NN)
    for k in range(8):
        core_tiles[pl.ds(k, RANK, stride=8), :] = product[:, 128 * k:128 * k + 128]

    def z_copy(d):
        to = wrap(f + d, NF)
        return remote(core_tiles.at[pl.ds(pl.multiple_of(to * 48, 8), 48), :],
                      core.at[pl.ds(pl.multiple_of(f * 48, 8), 48), :],
                      s_z.at[d], r_z.at[d], {"fibre": to})

    for d in range(1, NF):
        z_copy(d).start()
    own_at = pl.ds(pl.multiple_of(f * 48, 8), 48)
    core_copy = pltpu.make_async_copy(core_tiles.at[own_at, :], core.at[own_at, :], s_o.at[0])
    core_copy.start()
    turned[...] = permuted(basis[...], permutation(True))[:, :I1]
    factor_copy = pltpu.make_async_copy(turned, factor, s_o.at[1])
    factor_copy.start()

    for d in range(1, NF):
        t_copy(d).wait_send()
        for k in range(3):
            x_copy(k, d).wait_send()
    a_copy.wait_send()
    a2_copy.wait_send()
    for d in range(1, NZ):
        c_copy(d).wait_send()
        d_copy(d).wait_send()
        c2_copy(d).wait_send()
    for d in range(1, NR):
        b_copy(d).wait_send()
        b2_copy(d).wait_send()
        e_copy(d).wait_send()
        e2_copy(d).wait_send()
    for d in range(NR):
        f_pass(d).wait_send()
        f2_pass(d).wait_send()
    for d in range(1, NF):
        z_copy(d).wait()
    core_copy.wait()
    factor_copy.wait()


def main_call(slab, start):
    dma = pltpu.SemaphoreType.DMA
    any_spec = pl.BlockSpec(memory_space=pl.ANY)

    def tiles(*shape):
        return pltpu.VMEM((*shape, 8, 128), F32)

    return pl.pallas_call(
        main_kernel,
        out_shape=(
            jax.ShapeDtypeStruct((RANK, I1), F32),
            jax.ShapeDtypeStruct((RANK * 8, 128), F32),
        ),
        in_specs=[any_spec, pl.BlockSpec(memory_space=pltpu.VMEM)],
        out_specs=(any_spec, any_spec),
        scratch_shapes=[
            pltpu.VMEM((PAD1, OWN), F32),
            pltpu.VMEM((PAD1, OWN), BF16),
            pltpu.VMEM((PAD1, OWN), BF16),
            pltpu.VMEM((8, COLS), F32),
            tiles(NF, 2), tiles(NF, 2),
            pltpu.VMEM((PAD1, PAD1), BF16),
            pltpu.VMEM((PAD1, PAD1), BF16),
            pltpu.VMEM((RANK, PAD1), F32),
            pltpu.VMEM((RANK, I1), F32),
            pltpu.VMEM((RANK * 8, 128), F32),
            tiles(2, NR, NZ), tiles(NR, NZ), tiles(NR, NZ), tiles(NR, NZ),
            tiles(NZ), tiles(NZ), tiles(), tiles(2, NR, NZ),
            tiles(2, NR, T3), tiles(NR, T3), tiles(NR, T3), tiles(NR, T3),
            tiles(T3), tiles(NZ, T3), tiles(2, NR, T3),
            dma((4,)),
            dma((4, NF)), dma((4, NF)),
            dma, dma,
            dma((NR,)), dma((NR,)),
            dma((NZ,)), dma((NZ,)),
            dma((NZ,)), dma((NZ,)),
            dma((NR,)), dma((NR,)),
            dma((NR,)), dma((NR,)),
            dma, dma,
            dma((NR,)), dma((NR,)),
            dma((NZ,)), dma((NZ,)),
            dma((NR,)), dma((NR,)),
            dma((NR,)), dma((NR,)),
            dma((NF,)), dma((NF,)),
            dma((2,)),
        ],
        compiler_params=pltpu.CompilerParams(
            collective_id=0, has_side_effects=True, vmem_limit_bytes=VMEM_LIMIT),
        name="main",
    )(slab, start)


def layout_kernel(turned, tiles, factor, core):
    factor[...] = turned[...]
    for s in range(NF):
        for k in range(8):
            core[:, pl.ds((8 * s + k) * 128, 128)] = tiles[pl.ds(48 * s + k, RANK // NF, stride=8), :]


def layout_call(turned, tiles):
    vmem = pl.BlockSpec(memory_space=pltpu.VMEM)
    return pl.pallas_call(
        layout_kernel,
        out_shape=(
            jax.ShapeDtypeStruct((RANK, I1), F32),
            jax.ShapeDtypeStruct((RANK // NF, COLS), F32),
        ),
        in_specs=[vmem, vmem],
        out_specs=(vmem, vmem),
        compiler_params=pltpu.CompilerParams(vmem_limit_bytes=VMEM_LIMIT),
        name="layout",
    )(turned, tiles)


def shards(slab, start_basis):
    factor, core = layout_call(*main_call(slab, start_basis.T))
    return factor.T, core


def solution(mesh):
    return jax.shard_map(
        shards,
        mesh=mesh,
        in_specs=(P("fibre", "rest"), P()),
        out_specs=(P(), P("fibre", "rest")),
        check_vma=False,
    )
```

```python
import jax
import jax.numpy as jnp
from jax import lax
from jax.experimental import pallas as pl
from jax.experimental.pallas import tpu as pltpu
from jax.sharding import PartitionSpec as P

ITERS = 3
HP = lax.Precision.HIGHEST
F32 = jnp.float32
BF16 = jnp.bfloat16
NF = 16
NR = 16
NZ = 8
ROWS = 42
I1 = 672
PAD1 = 768
RANK = 96
COLS = 16384
OWN = 1024
VMEM_LIMIT = 56 * 1024 * 1024

NT = (((1,), (1,)), ((), ()))
NN = (((1,), (0,)), ((), ()))


def split(x):
    hi = x.astype(BF16)
    lo = (x - hi.astype(F32)).astype(BF16)
    return hi, lo


def dot3(a, b, dims):
    ah, al = a
    bh, bl = b

    def d(u, v):
        return lax.dot_general(u, v, dims, preferred_element_type=F32)

    return d(ah, bh) + (d(ah, bl) + d(al, bh))


def remote(src, dst, send, recv, device):
    return pltpu.make_async_remote_copy(
        src_ref=src, dst_ref=dst, send_sem=send, recv_sem=recv,
        device_id=device, device_id_type=pl.DeviceIdType.MESH,
    )


def wrap(v, n):
    return lax.rem(v + n, n)


def inverse_factor(small):
    count = RANK // 8
    tiles = [small[8 * t:8 * t + 8] for t in range(count)]
    lane = lax.broadcasted_iota(jnp.int32, (8, 128), 1)
    sub = lax.broadcasted_iota(jnp.int32, (8, 128), 0)

    def over_lanes(v, j):
        return jnp.broadcast_to(v[:, j:j + 1], (8, 128))

    def over_rows(v, k):
        return jnp.broadcast_to(v[k:k + 1, :], (8, 128))

    out = []
    for t in range(count):
        v = tiles[t]
        cols = [over_lanes(v, 8 * t + k) for k in range(8)]
        below = [[over_lanes(tiles[r], 8 * t + k) for k in range(8)] for r in range(t + 1, count)]
        kept = jnp.zeros((8, 128), F32)
        pivots = jnp.ones((8, 128), F32)
        for k in range(8):
            at = sub == k
            here = lane == 8 * t + k
            pivot = over_rows(cols[k], k)
            inv = 1.0 / pivot
            row = jnp.where(here, 1.0, over_rows(v, k))
            kept = jnp.where(at, row, kept)
            pivots = jnp.where(at, pivot, pivots)
            scaled = row * inv
            v = jnp.where(at, scaled, jnp.where(here, 0.0, v) - cols[k] * scaled)
            for m in range(k + 1, 8):
                entry = over_rows(cols[m], k) * inv
                cols[m] = jnp.where(at, entry, cols[m] - cols[k] * entry)
        rows = [over_rows(v, k) for k in range(8)]
        block = (lane >= 8 * t) & (lane < 8 * t + 8)
        for r in range(t + 1, count):
            p = [below[r - t - 1][k] * rows[k] for k in range(8)]
            total = ((p[0] + p[1]) + (p[2] + p[3])) + ((p[4] + p[5]) + (p[6] + p[7]))
            tiles[r] = jnp.where(block, 0.0, tiles[r]) - total
        out.append(jnp.where(lane <= sub + 8 * t, kept * lax.rsqrt(pivots), 0.0))
    return jnp.concatenate(out, axis=0)


def permutation(transposed):
    p = lax.broadcasted_iota(jnp.int32, (PAD1, PAD1), 0 if transposed else 1)
    i = lax.broadcasted_iota(jnp.int32, (PAD1, PAD1), 1 if transposed else 0)
    q = p - ROW_T
    wide = ROWS * ((p & 255) >> 4) + (p & 15) + jnp.where(p >= ROW_B, 16, 0)
    narrow = ROWS * ((p - ROW_C) >> 3) + 32 + (p & 7)
    rest = ROWS * (q & 15) + 40 + (q >> 4)
    row = jnp.where(p < ROW_C, wide, jnp.where(p < ROW_T, narrow, jnp.where(p < I1, rest, p)))
    return jnp.where(row == i, 1.0, 0.0).astype(BF16)


def permuted(x, ones):
    hi = x.astype(BF16)
    left = x - hi.astype(F32)
    mid = left.astype(BF16)
    low = (left - mid.astype(F32)).astype(BF16)

    def d(u):
        return lax.dot_general(u, ones, NN, preferred_element_type=F32)

    return d(hi) + (d(mid) + d(low))


ROW_B, ROW_C, ROW_T = 256, 512, 640
BATCHES = (
    [(0, 0), (1, 0), (1, 1), (5, 0), (5, 1), (5, 5)],
    [(2, 0), (2, 1), (2, 2), (3, 0), (3, 1), (3, 2), (3, 3), (5, 2), (5, 3)],
    [(4, 0), (4, 1), (4, 2), (4, 3), (4, 4), (5, 4)],
)
SLOTS = (2, 4, 3)


def block_rows(i):
    return 32 if i == 5 else 128


def far(step, size):
    return min(step, size - step)


ALONG_Z = sorted([(dz, dc) for dz in range(NZ) for dc in range(2) if dz or dc], key=lambda o: (-far(o[0], NZ), o[1], o[0]))
ACROSS = sorted([(dx, dy) for dx in range(4) for dy in range(4) if dx or dy], key=lambda o: (-far(o[0], 4) - far(o[1], 4), o))
SEM_B, SEM_Z, SEM_E, SEM_F, SEMS = 1, 17, 25, 41, 57


def mesh_signal(sem, device):
    pl.semaphore_signal(sem, inc=1, device_id=device, device_id_type=pl.DeviceIdType.MESH)


class Sum:
    def __init__(self, batch, refs, sems, send, f, r):
        self.count = SLOTS[batch]
        self.part, self.ra, self.sa, self.rb, self.own, self.rz, self.full = refs
        self.sems = sems.at[batch]
        self.send = send
        self.r, self.z, self.c = r, f // 2, lax.rem(f, 2)
        self.other = {"fibre": self.z * 2 + (1 - self.c)}
        self.tiles = {}
        at = 0
        for i, j in BATCHES[batch]:
            self.tiles[i, j] = at
            at += block_rows(i) // 8
        for n in range(at, 2 * NR * self.count):
            self.part[self.index(n)] = jnp.zeros((8, 128), F32)

    def index(self, n):
        return n // (NR * self.count), (n // self.count) % NR, n % self.count

    def put(self, i, j, value):
        for k in range(block_rows(i) // 8):
            self.part[self.index(self.tiles[i, j] + k)] = value[8 * k:8 * k + 8]

    def get(self, i, j):
        first = self.tiles[i, j]
        return jnp.concatenate([self.full[self.index(first + k)] for k in range(block_rows(i) // 8)], axis=0)

    def copy(self, src, dst, sem, device):
        return remote(src, dst, self.sems.at[0, sem], self.sems.at[1, sem], device)

    def rest(self, offset, sign=1):
        x, y = self.r // 4, lax.rem(self.r, 4)
        return wrap(x + sign * offset[0], 4) * 4 + wrap(y + sign * offset[1], 4)

    def a(self):
        return self.copy(self.part.at[1 - self.c], self.ra, 0, self.other)

    def b(self, o):
        to = self.rest(o)
        k = 4 * o[0] + o[1]
        return self.copy(self.sa.at[to], self.rb.at[k], SEM_B + k, {"rest": to})

    def along(self, d):
        return self.copy(self.own, self.rz.at[self.z], SEM_Z + d, {"fibre": wrap(self.z + d, NZ) * 2 + self.c})

    def e(self, o):
        mine = self.full.at[self.c, self.r]
        return self.copy(mine, mine, SEM_E + 4 * o[0] + o[1], {"rest": self.rest(o)})

    def f(self, o):
        piece = self.full.at[self.c, self.rest(o, -1)]
        return self.copy(piece, piece, SEM_F + 4 * o[0] + o[1], self.other)

    def start(self):
        self.send(self.a())

    def spread(self):
        self.a().wait_recv()
        self.sa[...] = self.part[self.c] + self.ra[...]
        for o in ACROSS:
            self.send(self.b(o))

    def up(self):
        total = self.sa[self.r]
        for o in ACROSS:
            self.b(o).wait_recv()
            total = total + self.rb[4 * o[0] + o[1]]
        self.own[...] = total
        self.rz[self.z] = total
        for d in (4, 3, 5, 2, 6, 1, 7):
            self.send(self.along(d))

    def back(self):
        for d in range(1, NZ):
            self.along(d).wait_recv()
        s = [self.rz[k] for k in range(NZ)]
        self.full[self.c, self.r] = ((s[0] + s[1]) + (s[2] + s[3])) + ((s[4] + s[5]) + (s[6] + s[7]))
        for o in ACROSS:
            self.send(self.e(o))
        self.send(self.f((0, 0)))

    def finish(self):
        for o in reversed(ACROSS):
            self.e(o).wait_recv()
            self.send(self.f(o))
        for o in [(0, 0)] + ACROSS:
            self.f(o).wait_recv()


def main_kernel(slab, start, factor, core, fc, fh, fl, tail, tail_out, tail_in, gh, gl, basis, turned, core_tiles,
                s_own, s_x, r_x, s_z, r_z, s_o, s_sum, *sum_refs):
    f = lax.axis_index("fibre")
    r = lax.axis_index("rest")
    z = f // 2
    c = lax.rem(f, 2)

    sent = []

    def send(copy):
        copy.start()
        sent.append(copy)

    barrier = pltpu.get_barrier_semaphore()
    for d in range(1, NF):
        mesh_signal(barrier, {"fibre": wrap(f + d, NF)})
    for d in range(1, NR):
        mesh_signal(barrier, {"rest": wrap(r + d, NR)})

    sets = [(0, 16, 0), (16, 16, ROW_B), (32, 8, ROW_C)]

    def partner(o):
        dz, dc = o
        return wrap(z + dz, NZ) * 2 + (c if dc == 0 else 1 - c)

    def piece(k, to):
        at, rows, _ = sets[k]
        return slab.at[pl.ds(at, rows), pl.ds(pl.multiple_of(to * OWN, OWN), OWN)]

    def place(k):
        _, rows, base = sets[k]
        return fc.at[pl.ds(pl.multiple_of(base + f * rows, rows), rows), :]

    def x_copy(k, o):
        to = partner(o)
        n = 2 * o[0] + o[1]
        return remote(piece(k, to), place(k), s_x.at[k, n], r_x.at[k, n], {"fibre": to})

    def t_copy(o):
        to = partner(o)
        n = 2 * o[0] + o[1]
        return remote(tail_out.at[to], tail_in.at[f], s_x.at[3, n], r_x.at[3, n], {"fibre": to})

    tail_copy = pltpu.make_async_copy(slab.at[pl.ds(40, 2), :], tail.at[pl.ds(0, 2), :], s_own.at[3])
    tail_copy.start()
    own_copies = [pltpu.make_async_copy(piece(k, f), place(k), s_own.at[k]) for k in range(3)]
    for copy in own_copies:
        copy.start()
    pl.semaphore_wait(barrier, NF - 1 + NR - 1)

    for o in ALONG_Z:
        send(x_copy(0, o))
    tail_copy.wait()
    for to in range(NF):
        for k in range(8):
            both = tail[0:2, pl.ds((to * 8 + k) * 128, 128)]
            tail_out[to, 0, k:k + 1, :] = both[0:1]
            tail_out[to, 1, k:k + 1, :] = both[1:2]
    tail_in[f] = tail_out[f]
    for o in ALONG_Z:
        send(t_copy(o))
    for k in (1, 2):
        for o in ALONG_Z:
            send(x_copy(k, o))

    sums = [Sum(k, sum_refs[7 * k:7 * k + 7], s_sum, send, f, r) for k in range(3)]

    def rounded(top, rows):
        at = pl.ds(top, rows)
        fh[at, :], fl[at, :] = split(fc[at, :])

    def pair(top, rows):
        return fh[pl.ds(top, rows), :], fl[pl.ds(top, rows), :]

    def wait_set(k):
        own_copies[k].wait()
        for o in ALONG_Z:
            x_copy(k, o).wait_recv()

    def put(batch, i0, value, j0=0):
        step = block_rows(i0)
        for i, j in BATCHES[batch]:
            top, left = (i - i0) * step, (j - j0) * 128
            if 0 <= top < value.shape[0] and 0 <= left < value.shape[1] and (i == 5) == (i0 == 5):
                sums[batch].put(i, j, value[top:top + step, left:left + 128])

    def unpack(batch):
        for i, j in BATCHES[batch]:
            value = sums[batch].get(i, j)
            if i == 5:
                value = jnp.concatenate([value, jnp.zeros((96, 128), F32)], axis=0)
            for at, v in [((i, j), value)] + ([((j, i), value.T)] if i != j else []):
                where = (pl.ds(at[0] * 128, 128), pl.ds(at[1] * 128, 128))
                gh[where], gl[where] = split(v)

    fc[pl.ds(I1, PAD1 - I1), :] = jnp.zeros((PAD1 - I1, OWN), F32)
    wide_start = jnp.concatenate([start[...], jnp.zeros((RANK, PAD1 - I1), F32)], axis=1)
    basis[...] = permuted(wide_start, permutation(False))

    wait_set(0)
    rounded(0, 256)
    put(0, 0, dot3(pair(0, 256), pair(0, 256), NT))
    for o in ALONG_Z:
        t_copy(o).wait_recv()
    for i in range(2):
        for k in range(8):
            fc[pl.ds(ROW_T + 16 * i, 16), pl.ds(128 * k, 128)] = jnp.concatenate(
                [tail_in[s, i, k:k + 1, :] for s in range(NF)], axis=0)
    rounded(ROW_T, PAD1 - ROW_T)
    put(0, 5, dot3(pair(ROW_T, 32), pair(0, 256), NT))
    put(0, 5, dot3(pair(ROW_T, 32), pair(ROW_T, 128), NT), 5)
    sums[0].start()
    sums[0].spread()
    sums[0].up()

    wait_set(1)
    rounded(ROW_B, 256)
    put(1, 2, dot3(pair(ROW_B, 256), pair(0, 512), NT))
    put(1, 5, dot3(pair(ROW_T, 32), pair(ROW_B, 256), NT), 2)
    sums[1].start()
    sums[1].spread()
    sums[1].up()

    wait_set(2)
    rounded(ROW_C, 128)
    put(2, 4, dot3(pair(ROW_C, 128), pair(0, 640), NT))
    put(2, 5, dot3(pair(ROW_T, 32), pair(ROW_C, 128), NT), 4)
    sums[2].start()
    sums[2].spread()
    sums[0].back()
    sums[1].back()
    sums[2].up()
    sums[0].finish()
    sums[1].finish()
    unpack(0)
    unpack(1)
    sums[2].back()
    sums[2].finish()
    unpack(2)

    def step(_, carry):
        image = dot3(split(basis[...]), (gh[...], gl[...]), NN)
        wide = jnp.concatenate([image, jnp.zeros((128 - RANK, PAD1), F32)], axis=0)
        small = lax.dot_general(image, wide, NT, precision=HP, preferred_element_type=F32)
        inverse = inverse_factor(small)[:, :RANK]
        basis[...] = lax.dot_general(inverse, image, NN, precision=HP, preferred_element_type=F32)
        return carry

    lax.fori_loop(0, ITERS, step, 0)

    product = dot3(split(basis[...]), (fh[...], fl[...]), NN)
    for k in range(8):
        core_tiles[pl.ds(k, RANK, stride=8), :] = product[:, 128 * k:128 * k + 128]

    def z_copy(o):
        to = partner(o)
        n = 2 * o[0] + o[1]
        return remote(core_tiles.at[pl.ds(pl.multiple_of(to * 48, 8), 48), :],
                      core.at[pl.ds(pl.multiple_of(f * 48, 8), 48), :],
                      s_z.at[n], r_z.at[n], {"fibre": to})

    for o in ALONG_Z:
        send(z_copy(o))
    own_at = pl.ds(pl.multiple_of(f * 48, 8), 48)
    core_copy = pltpu.make_async_copy(core_tiles.at[own_at, :], core.at[own_at, :], s_o.at[0])
    core_copy.start()
    turned[...] = permuted(basis[...], permutation(True))[:, :I1]
    factor_copy = pltpu.make_async_copy(turned, factor, s_o.at[1])
    factor_copy.start()

    for o in ALONG_Z:
        z_copy(o).wait_recv()
    for copy in sent:
        copy.wait_send()
    core_copy.wait()
    factor_copy.wait()


def main_call(slab, start):
    dma = pltpu.SemaphoreType.DMA
    any_spec = pl.BlockSpec(memory_space=pl.ANY)

    def tiles(*shape):
        return pltpu.VMEM((*shape, 8, 128), F32)

    sum_scratch = []
    for n in SLOTS:
        sum_scratch += [tiles(2, NR, n), tiles(NR, n), tiles(NR, n), tiles(NR, n), tiles(n), tiles(NZ, n), tiles(2, NR, n)]
    return pl.pallas_call(
        main_kernel,
        out_shape=(
            jax.ShapeDtypeStruct((RANK, I1), F32),
            jax.ShapeDtypeStruct((RANK * 8, 128), F32),
        ),
        in_specs=[any_spec, pl.BlockSpec(memory_space=pltpu.VMEM)],
        out_specs=(any_spec, any_spec),
        scratch_shapes=[
            pltpu.VMEM((PAD1, OWN), F32),
            pltpu.VMEM((PAD1, OWN), BF16),
            pltpu.VMEM((PAD1, OWN), BF16),
            pltpu.VMEM((8, COLS), F32),
            tiles(NF, 2), tiles(NF, 2),
            pltpu.VMEM((PAD1, PAD1), BF16),
            pltpu.VMEM((PAD1, PAD1), BF16),
            pltpu.VMEM((RANK, PAD1), F32),
            pltpu.VMEM((RANK, I1), F32),
            pltpu.VMEM((RANK * 8, 128), F32),
            dma((4,)),
            dma((4, NF)), dma((4, NF)),
            dma((NF,)), dma((NF,)),
            dma((2,)),
            dma((3, 2, SEMS)),
        ] + sum_scratch,
        compiler_params=pltpu.CompilerParams(
            collective_id=0, has_side_effects=True, vmem_limit_bytes=VMEM_LIMIT),
        name="main",
    )(slab, start)


def layout_kernel(turned, tiles, factor, core):
    factor[...] = turned[...]
    for s in range(NF):
        for k in range(8):
            core[:, pl.ds((8 * s + k) * 128, 128)] = tiles[pl.ds(48 * s + k, RANK // NF, stride=8), :]


def layout_call(turned, tiles):
    vmem = pl.BlockSpec(memory_space=pltpu.VMEM)
    return pl.pallas_call(
        layout_kernel,
        out_shape=(
            jax.ShapeDtypeStruct((RANK, I1), F32),
            jax.ShapeDtypeStruct((RANK // NF, COLS), F32),
        ),
        in_specs=[vmem, vmem],
        out_specs=(vmem, vmem),
        compiler_params=pltpu.CompilerParams(vmem_limit_bytes=VMEM_LIMIT),
        name="layout",
    )(turned, tiles)


def shards(slab, start_basis):
    factor, core = layout_call(*main_call(slab, start_basis.T))
    return factor.T, core


def solution(mesh):
    return jax.shard_map(
        shards,
        mesh=mesh,
        in_specs=(P("fibre", "rest"), P()),
        out_specs=(P(), P("fibre", "rest")),
        check_vma=False,
    )
```

```python
import jax
import jax.numpy as jnp
from jax import lax
from jax.experimental import pallas as pl
from jax.experimental.pallas import tpu as pltpu
from jax.sharding import PartitionSpec as P

ITERS = 3
HP = lax.Precision.HIGHEST
F32 = jnp.float32
BF16 = jnp.bfloat16
NF = 16
NR = 16
NZ = 8
ROWS = 42
I1 = 672
PAD1 = 768
RANK = 96
COLS = 16384
OWN = 1024
VMEM_LIMIT = 56 * 1024 * 1024

NT = (((1,), (1,)), ((), ()))
NN = (((1,), (0,)), ((), ()))


def split(x):
    hi = x.astype(BF16)
    lo = (x - hi.astype(F32)).astype(BF16)
    return hi, lo


def dot3(a, b, dims):
    ah, al = a
    bh, bl = b

    def d(u, v):
        return lax.dot_general(u, v, dims, preferred_element_type=F32)

    return d(ah, bh) + (d(ah, bl) + d(al, bh))


def remote(src, dst, send, recv, device):
    return pltpu.make_async_remote_copy(
        src_ref=src, dst_ref=dst, send_sem=send, recv_sem=recv,
        device_id=device, device_id_type=pl.DeviceIdType.MESH,
    )


def wrap(v, n):
    return lax.rem(v + n, n)


def inverse_factor(small, beside):
    count = RANK // 8
    width = 16
    span = width // 8
    tiles = [small[8 * t:8 * t + 8] for t in range(count)]
    lane = lax.broadcasted_iota(jnp.int32, (8, 128), 1)
    sub = lax.broadcasted_iota(jnp.int32, (8, 128), 0)

    def over_lanes(v, j):
        return jnp.broadcast_to(v[:, j:j + 1], (8, 128))

    def over_rows(v, k):
        return jnp.broadcast_to(v[k:k + 1, :], (8, 128))

    out = []
    for t in range(0, count, span):
        first = 8 * t
        v = tiles[t:t + span]
        cols = [[over_lanes(u, first + k) for u in v] for k in range(width)]
        if t // span < len(beside):
            beside[t // span]()
        kept = [jnp.zeros((8, 128), F32) for _ in v]
        pivots = [jnp.ones((8, 128), F32) for _ in v]
        for k in range(width):
            w, i = divmod(k, 8)
            at = sub == i
            here = lane == first + k
            pivot = over_rows(cols[k][w], i)
            inv = 1.0 / pivot
            row = jnp.where(here, 1.0, over_rows(v[w], i))
            kept[w] = jnp.where(at, row, kept[w])
            pivots[w] = jnp.where(at, pivot, pivots[w])
            times = [jnp.where(at, -1.0, u) if n == w else u for n, u in enumerate(cols[k])]
            for n in range(span):
                clear = (here | at) if n == w else here
                v[n] = jnp.where(clear, 0.0, v[n]) - (times[n] * row) * inv
            for m in range(k + 1, width):
                entry = over_rows(cols[m][w], i)
                for n in range(span):
                    base = jnp.where(at, 0.0, cols[m][n]) if n == w else cols[m][n]
                    cols[m][n] = base - (times[n] * entry) * inv
        rows = [over_rows(v[k // 8], k % 8) for k in range(width)]
        block = (lane >= first) & (lane < first + width)
        for r in range(t + span, count):
            p = [over_lanes(tiles[r], first + k) * rows[k] for k in range(width)]
            while len(p) > 1:
                p = [p[n] + p[n + 1] for n in range(0, len(p), 2)]
            tiles[r] = jnp.where(block, 0.0, tiles[r]) - p[0]
        for n in range(span):
            out.append(jnp.where(lane <= sub + 8 * (t + n), kept[n] * lax.rsqrt(pivots[n]), 0.0))
    return jnp.concatenate(out, axis=0)


def permutation(transposed):
    p = lax.broadcasted_iota(jnp.int32, (PAD1, PAD1), 0 if transposed else 1)
    i = lax.broadcasted_iota(jnp.int32, (PAD1, PAD1), 1 if transposed else 0)
    q = p - ROW_T
    wide = ROWS * ((p & 255) >> 4) + (p & 15) + jnp.where(p >= ROW_B, 16, 0)
    narrow = ROWS * ((p - ROW_C) >> 3) + 32 + (p & 7)
    rest = ROWS * (q & 15) + 40 + (q >> 4)
    row = jnp.where(p < ROW_C, wide, jnp.where(p < ROW_T, narrow, jnp.where(p < I1, rest, p)))
    return jnp.where(row == i, 1.0, 0.0).astype(BF16)


def permuted(x, ones):
    hi = x.astype(BF16)
    left = x - hi.astype(F32)
    mid = left.astype(BF16)
    low = (left - mid.astype(F32)).astype(BF16)

    def d(u):
        return lax.dot_general(u, ones, NN, preferred_element_type=F32)

    return d(hi) + (d(mid) + d(low))


ROW_B, ROW_C, ROW_T = 256, 512, 640
BATCHES = (
    [(0, 0), (1, 0), (1, 1), (5, 0), (5, 1), (5, 5)],
    [(2, 0), (2, 1), (2, 2), (3, 0), (3, 1), (3, 2), (3, 3), (5, 2), (5, 3)],
    [(4, 0), (4, 1), (4, 2), (4, 3), (4, 4), (5, 4)],
)
SLOTS = (2, 4, 3)


def block_rows(i):
    return 32 if i == 5 else 128


def far(step, size):
    return min(step, size - step)


ALONG_Z = sorted([(dz, dc) for dz in range(NZ) for dc in range(2) if dz or dc], key=lambda o: (-far(o[0], NZ), o[1], o[0]))
ACROSS = sorted([(dx, dy) for dx in range(4) for dy in range(4) if dx or dy], key=lambda o: (-far(o[0], 4) - far(o[1], 4), o))
SEM_B, SEM_Z, SEM_E, SEM_F, SEMS = 1, 17, 25, 41, 42


def mesh_signal(sem, device):
    pl.semaphore_signal(sem, inc=1, device_id=device, device_id_type=pl.DeviceIdType.MESH)


class Sum:
    def __init__(self, batch, refs, sems, send, f, r):
        self.count = SLOTS[batch]
        self.part, self.ra, self.sa, self.rb, self.own, self.rz, self.full = refs
        self.sems = sems.at[batch]
        self.send = send
        self.r, self.z, self.c = r, f // 2, lax.rem(f, 2)
        self.other = {"fibre": self.z * 2 + (1 - self.c)}
        self.tiles = {}
        at = 0
        for i, j in BATCHES[batch]:
            self.tiles[i, j] = at
            at += block_rows(i) // 8
        for n in range(at, 2 * NR * self.count):
            self.part[self.index(n)] = jnp.zeros((8, 128), F32)

    def index(self, n):
        return n // (NR * self.count), (n // self.count) % NR, n % self.count

    def put(self, i, j, value):
        for k in range(block_rows(i) // 8):
            self.part[self.index(self.tiles[i, j] + k)] = value[8 * k:8 * k + 8]

    def get(self, i, j):
        first = self.tiles[i, j]
        return jnp.concatenate([self.full[self.index(first + k)] for k in range(block_rows(i) // 8)], axis=0)

    def copy(self, src, dst, sem, device):
        return remote(src, dst, self.sems.at[0, sem], self.sems.at[1, sem], device)

    def rest(self, offset, sign=1):
        x, y = self.r // 4, lax.rem(self.r, 4)
        return wrap(x + sign * offset[0], 4) * 4 + wrap(y + sign * offset[1], 4)

    def a(self):
        return self.copy(self.part.at[1 - self.c], self.ra, 0, self.other)

    def b(self, o):
        to = self.rest(o)
        k = 4 * o[0] + o[1]
        return self.copy(self.sa.at[to], self.rb.at[k], SEM_B + k, {"rest": to})

    def along(self, d):
        return self.copy(self.own, self.rz.at[self.z], SEM_Z + d, {"fibre": wrap(self.z + d, NZ) * 2 + self.c})

    def e(self, o):
        mine = self.full.at[self.c, self.r]
        return self.copy(mine, mine, SEM_E + 4 * o[0] + o[1], {"rest": self.rest(o)})

    def start(self):
        self.send(self.a())

    def spread(self):
        self.a().wait_recv()
        self.sa[...] = self.part[self.c] + self.ra[...]
        for o in ACROSS:
            self.send(self.b(o))

    def up(self):
        total = self.sa[self.r]
        for o in ACROSS:
            self.b(o).wait_recv()
            total = total + self.rb[4 * o[0] + o[1]]
        self.own[...] = total
        self.rz[self.z] = total
        for d in (4, 3, 5, 2, 6, 1, 7):
            self.send(self.along(d))

    def back(self):
        for d in range(1, NZ):
            self.along(d).wait_recv()
        s = [self.rz[k] for k in range(NZ)]
        self.full[self.c, self.r] = ((s[0] + s[1]) + (s[2] + s[3])) + ((s[4] + s[5]) + (s[6] + s[7]))
        for o in ACROSS:
            self.send(self.e(o))

    def finish(self):
        for o in ACROSS:
            self.e(o).wait_recv()
        half = self.full.at[self.c]
        copy = self.copy(half, half, SEM_F, self.other)
        self.send(copy)
        copy.wait_recv()


def main_kernel(slab, start, factor, core, fc, fh, fl, tail, tail_out, tail_in, gh, gl, basis, ahead, turned, core_tiles,
                s_own, s_x, r_x, s_z, r_z, s_o, s_sum, *sum_refs):
    f = lax.axis_index("fibre")
    r = lax.axis_index("rest")
    z = f // 2
    c = lax.rem(f, 2)

    sent = []

    def send(copy):
        copy.start()
        sent.append(copy)

    barrier = pltpu.get_barrier_semaphore()
    for d in range(1, NF):
        mesh_signal(barrier, {"fibre": wrap(f + d, NF)})
    for d in range(1, NR):
        mesh_signal(barrier, {"rest": wrap(r + d, NR)})

    sets = [(0, 16, 0), (16, 16, ROW_B), (32, 8, ROW_C)]

    def partner(o):
        dz, dc = o
        return wrap(z + dz, NZ) * 2 + (c if dc == 0 else 1 - c)

    def piece(k, to):
        at, rows, _ = sets[k]
        return slab.at[pl.ds(at, rows), pl.ds(pl.multiple_of(to * OWN, OWN), OWN)]

    def place(k):
        _, rows, base = sets[k]
        return fc.at[pl.ds(pl.multiple_of(base + f * rows, rows), rows), :]

    def x_copy(k, o):
        to = partner(o)
        n = 2 * o[0] + o[1]
        return remote(piece(k, to), place(k), s_x.at[k, n], r_x.at[k, n], {"fibre": to})

    def t_copy(o):
        to = partner(o)
        n = 2 * o[0] + o[1]
        return remote(tail_out.at[to], tail_in.at[f], s_x.at[3, n], r_x.at[3, n], {"fibre": to})

    tail_copy = pltpu.make_async_copy(slab.at[pl.ds(40, 2), :], tail.at[pl.ds(0, 2), :], s_own.at[3])
    tail_copy.start()
    own_copies = [pltpu.make_async_copy(piece(k, f), place(k), s_own.at[k]) for k in range(3)]
    for copy in own_copies:
        copy.start()
    pl.semaphore_wait(barrier, NF - 1 + NR - 1)

    for o in ALONG_Z:
        send(x_copy(0, o))
    tail_copy.wait()
    for to in range(NF):
        for k in range(8):
            both = tail[0:2, pl.ds((to * 8 + k) * 128, 128)]
            tail_out[to, 0, k:k + 1, :] = both[0:1]
            tail_out[to, 1, k:k + 1, :] = both[1:2]
    tail_in[f] = tail_out[f]
    for o in ALONG_Z:
        send(t_copy(o))
    for k in (1, 2):
        for o in ALONG_Z:
            send(x_copy(k, o))

    sums = [Sum(k, sum_refs[7 * k:7 * k + 7], s_sum, send, f, r) for k in range(3)]

    def rounded(top, rows):
        at = pl.ds(top, rows)
        fh[at, :], fl[at, :] = split(fc[at, :])

    def pair(top, rows):
        return fh[pl.ds(top, rows), :], fl[pl.ds(top, rows), :]

    def wait_set(k):
        own_copies[k].wait()
        for o in ALONG_Z:
            x_copy(k, o).wait_recv()

    def put(batch, i0, value, j0=0):
        step = block_rows(i0)
        for i, j in BATCHES[batch]:
            top, left = (i - i0) * step, (j - j0) * 128
            if 0 <= top < value.shape[0] and 0 <= left < value.shape[1] and (i == 5) == (i0 == 5):
                sums[batch].put(i, j, value[top:top + step, left:left + 128])

    def unpack(batch):
        for i, j in BATCHES[batch]:
            value = sums[batch].get(i, j)
            if i == 5:
                value = jnp.concatenate([value, jnp.zeros((96, 128), F32)], axis=0)
            for at, v in [((i, j), value)] + ([((j, i), value.T)] if i != j else []):
                where = (pl.ds(at[0] * 128, 128), pl.ds(at[1] * 128, 128))
                gh[where], gl[where] = split(v)

    fc[pl.ds(I1, PAD1 - I1), :] = jnp.zeros((PAD1 - I1, OWN), F32)
    wide_start = jnp.concatenate([start[...], jnp.zeros((RANK, PAD1 - I1), F32)], axis=1)
    basis[...] = permuted(wide_start, permutation(False))

    wait_set(0)
    rounded(0, 256)
    put(0, 0, dot3(pair(0, 256), pair(0, 256), NT))
    for o in ALONG_Z:
        t_copy(o).wait_recv()
    for i in range(2):
        for k in range(8):
            fc[pl.ds(ROW_T + 16 * i, 16), pl.ds(128 * k, 128)] = jnp.concatenate(
                [tail_in[s, i, k:k + 1, :] for s in range(NF)], axis=0)
    rounded(ROW_T, PAD1 - ROW_T)
    put(0, 5, dot3(pair(ROW_T, 32), pair(0, 256), NT))
    put(0, 5, dot3(pair(ROW_T, 32), pair(ROW_T, 128), NT), 5)
    sums[0].start()
    sums[0].spread()
    sums[0].up()

    wait_set(1)
    rounded(ROW_B, 256)
    put(1, 2, dot3(pair(ROW_B, 256), pair(0, 512), NT))
    put(1, 5, dot3(pair(ROW_T, 32), pair(ROW_B, 256), NT), 2)
    sums[1].start()
    sums[1].spread()
    sums[1].up()

    wait_set(2)
    rounded(ROW_C, 128)
    put(2, 4, dot3(pair(ROW_C, 128), pair(0, 640), NT))
    put(2, 5, dot3(pair(ROW_T, 32), pair(ROW_C, 128), NT), 4)
    sums[2].start()
    sums[2].spread()
    sums[0].back()
    sums[2].up()
    sums[1].back()
    sums[2].back()
    sums[0].finish()
    sums[1].finish()
    unpack(0)
    unpack(1)
    sums[2].finish()
    unpack(2)

    def exact(u, v):
        return lax.dot_general(u, v, NN, precision=HP, preferred_element_type=F32)

    def beside_factor(high, low, width):
        image = basis[...]
        parts = split(image)
        wide = jnp.concatenate([image, jnp.zeros((128 - RANK, PAD1), F32)], axis=0)
        small = lax.dot_general(image, wide, NT, precision=HP, preferred_element_type=F32)

        def piece(at):
            def work():
                ahead[:, at] = dot3(parts, (high[:, at], low[:, at]), NN)
            return work

        work = [piece(pl.ds(k, 256)) for k in range(0, width, 256)]
        return inverse_factor(small, work)[:, :RANK]

    basis[...] = dot3(split(basis[...]), (gh[...], gl[...]), NN)

    def step(_, carry):
        inverse = beside_factor(gh, gl, PAD1)
        basis[...] = exact(inverse, ahead[:, pl.ds(0, PAD1)])
        return carry

    lax.fori_loop(0, ITERS - 1, step, 0)
    inverse = beside_factor(fh, fl, OWN)

    product = exact(inverse, ahead[...])
    for k in range(8):
        core_tiles[pl.ds(k, RANK, stride=8), :] = product[:, 128 * k:128 * k + 128]

    def z_copy(o):
        to = partner(o)
        n = 2 * o[0] + o[1]
        return remote(core_tiles.at[pl.ds(pl.multiple_of(to * 48, 8), 48), :],
                      core.at[pl.ds(pl.multiple_of(f * 48, 8), 48), :],
                      s_z.at[n], r_z.at[n], {"fibre": to})

    for o in ALONG_Z:
        send(z_copy(o))
    own_at = pl.ds(pl.multiple_of(f * 48, 8), 48)
    core_copy = pltpu.make_async_copy(core_tiles.at[own_at, :], core.at[own_at, :], s_o.at[0])
    core_copy.start()
    turned[...] = permuted(exact(inverse, basis[...]), permutation(True))[:, :I1]
    factor_copy = pltpu.make_async_copy(turned, factor, s_o.at[1])
    factor_copy.start()

    for o in ALONG_Z:
        z_copy(o).wait_recv()
    for copy in sent:
        copy.wait_send()
    core_copy.wait()
    factor_copy.wait()


def main_call(slab, start):
    dma = pltpu.SemaphoreType.DMA
    any_spec = pl.BlockSpec(memory_space=pl.ANY)

    def tiles(*shape):
        return pltpu.VMEM((*shape, 8, 128), F32)

    sum_scratch = []
    for n in SLOTS:
        sum_scratch += [tiles(2, NR, n), tiles(NR, n), tiles(NR, n), tiles(NR, n), tiles(n), tiles(NZ, n), tiles(2, NR, n)]
    return pl.pallas_call(
        main_kernel,
        out_shape=(
            jax.ShapeDtypeStruct((RANK, I1), F32),
            jax.ShapeDtypeStruct((RANK * 8, 128), F32),
        ),
        in_specs=[any_spec, pl.BlockSpec(memory_space=pltpu.VMEM)],
        out_specs=(any_spec, any_spec),
        scratch_shapes=[
            pltpu.VMEM((PAD1, OWN), F32),
            pltpu.VMEM((PAD1, OWN), BF16),
            pltpu.VMEM((PAD1, OWN), BF16),
            pltpu.VMEM((8, COLS), F32),
            tiles(NF, 2), tiles(NF, 2),
            pltpu.VMEM((PAD1, PAD1), BF16),
            pltpu.VMEM((PAD1, PAD1), BF16),
            pltpu.VMEM((RANK, PAD1), F32),
            pltpu.VMEM((RANK, OWN), F32),
            pltpu.VMEM((RANK, I1), F32),
            pltpu.VMEM((RANK * 8, 128), F32),
            dma((4,)),
            dma((4, NF)), dma((4, NF)),
            dma((NF,)), dma((NF,)),
            dma((2,)),
            dma((3, 2, SEMS)),
        ] + sum_scratch,
        compiler_params=pltpu.CompilerParams(
            collective_id=0, has_side_effects=True, vmem_limit_bytes=VMEM_LIMIT),
        name="main",
    )(slab, start)


def layout_kernel(turned, tiles, factor, core):
    factor[...] = turned[...]
    for s in range(NF):
        for k in range(8):
            core[:, pl.ds((8 * s + k) * 128, 128)] = tiles[pl.ds(48 * s + k, RANK // NF, stride=8), :]


def layout_call(turned, tiles):
    vmem = pl.BlockSpec(memory_space=pltpu.VMEM)
    return pl.pallas_call(
        layout_kernel,
        out_shape=(
            jax.ShapeDtypeStruct((RANK, I1), F32),
            jax.ShapeDtypeStruct((RANK // NF, COLS), F32),
        ),
        in_specs=[vmem, vmem],
        out_specs=(vmem, vmem),
        compiler_params=pltpu.CompilerParams(vmem_limit_bytes=VMEM_LIMIT),
        name="layout",
    )(turned, tiles)


def shards(slab, start_basis):
    factor, core = layout_call(*main_call(slab, start_basis.T))
    return factor.T, core


def solution(mesh):
    return jax.shard_map(
        shards,
        mesh=mesh,
        in_specs=(P("fibre", "rest"), P()),
        out_specs=(P(), P("fibre", "rest")),
        check_vma=False,
    )
```

```python
import jax
import jax.numpy as jnp
from jax import lax
from jax.experimental import pallas as pl
from jax.experimental.pallas import tpu as pltpu
from jax.sharding import PartitionSpec as P

ITERS = 3
HP = lax.Precision.HIGHEST
F32 = jnp.float32
BF16 = jnp.bfloat16
NF = 16
NR = 16
NZ = 8
ROWS = 42
I1 = 672
PAD1 = 768
RANK = 96
COLS = 16384
OWN = 1024
VMEM_LIMIT = 56 * 1024 * 1024

NT = (((1,), (1,)), ((), ()))
NN = (((1,), (0,)), ((), ()))


def split(x):
    hi = x.astype(BF16)
    lo = (x - hi.astype(F32)).astype(BF16)
    return hi, lo


def dot3(a, b, dims):
    ah, al = a
    bh, bl = b

    def d(u, v):
        return lax.dot_general(u, v, dims, preferred_element_type=F32)

    both = d(jnp.concatenate([ah, al], axis=0), bh)
    rows = ah.shape[0]
    return both[:rows] + (d(ah, bl) + both[rows:])


def remote(src, dst, send, recv, device):
    return pltpu.make_async_remote_copy(
        src_ref=src, dst_ref=dst, send_sem=send, recv_sem=recv,
        device_id=device, device_id_type=pl.DeviceIdType.MESH,
    )


def wrap(v, n):
    return lax.rem(v + n, n)


def inverse_factor(small, beside):
    count = RANK // 8
    width = 16
    span = width // 8
    tiles = [small[8 * t:8 * t + 8] for t in range(count)]
    lane = lax.broadcasted_iota(jnp.int32, (8, 128), 1)
    sub = lax.broadcasted_iota(jnp.int32, (8, 128), 0)

    def over_lanes(v, j):
        return jnp.broadcast_to(v[:, j:j + 1], (8, 128))

    def over_rows(v, k):
        return jnp.broadcast_to(v[k:k + 1, :], (8, 128))

    out = []
    for t in range(0, count, span):
        first = 8 * t
        v = tiles[t:t + span]
        cols = [[over_lanes(u, first + k) for u in v] for k in range(width)]
        if t // span < len(beside):
            beside[t // span]()
        kept = [jnp.zeros((8, 128), F32) for _ in v]
        pivots = [jnp.ones((8, 128), F32) for _ in v]
        for k in range(width):
            w, i = divmod(k, 8)
            at = sub == i
            here = lane == first + k
            pivot = over_rows(cols[k][w], i)
            inv = 1.0 / pivot
            row = jnp.where(here, 1.0, over_rows(v[w], i))
            kept[w] = jnp.where(at, row, kept[w])
            pivots[w] = jnp.where(at, pivot, pivots[w])
            times = [jnp.where(at, -1.0, u) if n == w else u for n, u in enumerate(cols[k])]
            for n in range(span):
                clear = (here | at) if n == w else here
                v[n] = jnp.where(clear, 0.0, v[n]) - (times[n] * row) * inv
            for m in range(k + 1, width):
                entry = over_rows(cols[m][w], i)
                for n in range(span):
                    base = jnp.where(at, 0.0, cols[m][n]) if n == w else cols[m][n]
                    cols[m][n] = base - (times[n] * entry) * inv
        rows = [over_rows(v[k // 8], k % 8) for k in range(width)]
        block = (lane >= first) & (lane < first + width)
        for r in range(t + span, count):
            p = [over_lanes(tiles[r], first + k) * rows[k] for k in range(width)]
            while len(p) > 1:
                p = [p[n] + p[n + 1] for n in range(0, len(p), 2)]
            tiles[r] = jnp.where(block, 0.0, tiles[r]) - p[0]
        for n in range(span):
            out.append(jnp.where(lane <= sub + 8 * (t + n), kept[n] * lax.rsqrt(pivots[n]), 0.0))
    return jnp.concatenate(out, axis=0)


def permutation(transposed):
    p = lax.broadcasted_iota(jnp.int32, (PAD1, PAD1), 0 if transposed else 1)
    i = lax.broadcasted_iota(jnp.int32, (PAD1, PAD1), 1 if transposed else 0)
    q = p - ROW_T
    wide = ROWS * ((p & 255) >> 4) + (p & 15) + jnp.where(p >= ROW_B, 16, 0)
    narrow = ROWS * ((p - ROW_C) >> 3) + 32 + (p & 7)
    rest = ROWS * (q & 15) + 40 + (q >> 4)
    row = jnp.where(p < ROW_C, wide, jnp.where(p < ROW_T, narrow, jnp.where(p < I1, rest, p)))
    return jnp.where(row == i, 1.0, 0.0).astype(BF16)


def permuted(x, ones):
    hi = x.astype(BF16)
    left = x - hi.astype(F32)
    mid = left.astype(BF16)
    low = (left - mid.astype(F32)).astype(BF16)

    def d(u):
        return lax.dot_general(u, ones, NN, preferred_element_type=F32)

    return d(hi) + (d(mid) + d(low))


ROW_B, ROW_C, ROW_T = 256, 512, 640
BATCHES = (
    [(0, 0), (1, 0), (1, 1)],
    [(2, 0), (2, 1), (2, 2), (3, 0), (3, 1), (3, 2), (3, 3)],
    [(4, 0), (4, 1), (4, 2), (4, 3), (4, 4)],
    [(5, 0), (5, 1), (5, 2), (5, 3), (5, 4), (5, 5)],
)
SLOTS = (2, 4, 3, 1)


def block_rows(i):
    return 32 if i == 5 else 128


def far(step, size):
    return min(step, size - step)


ALONG_Z = sorted([(dz, dc) for dz in range(NZ) for dc in range(2) if dz or dc], key=lambda o: (-far(o[0], NZ), o[1], o[0]))
ACROSS = sorted([(dx, dy) for dx in range(4) for dy in range(4) if dx or dy], key=lambda o: (-far(o[0], 4) - far(o[1], 4), o))
SEM_B, SEM_Z, SEM_E, SEM_F, SEMS = 1, 17, 25, 41, 42


def mesh_signal(sem, device):
    pl.semaphore_signal(sem, inc=1, device_id=device, device_id_type=pl.DeviceIdType.MESH)


class Sum:
    def __init__(self, batch, refs, sems, send, f, r):
        self.count = SLOTS[batch]
        self.part, self.ra, self.sa, self.rb, self.own, self.rz, self.full = refs
        self.sems = sems.at[batch]
        self.send = send
        self.r, self.z, self.c = r, f // 2, lax.rem(f, 2)
        self.other = {"fibre": self.z * 2 + (1 - self.c)}
        self.tiles = {}
        at = 0
        for i, j in BATCHES[batch]:
            self.tiles[i, j] = at
            at += block_rows(i) // 8
        for n in range(at, 2 * NR * self.count):
            self.part[self.index(n)] = jnp.zeros((8, 128), F32)

    def index(self, n):
        return n // (NR * self.count), (n // self.count) % NR, n % self.count

    def put(self, i, j, value):
        for k in range(block_rows(i) // 8):
            self.part[self.index(self.tiles[i, j] + k)] = value[8 * k:8 * k + 8]

    def get(self, i, j):
        first = self.tiles[i, j]
        return jnp.concatenate([self.full[self.index(first + k)] for k in range(block_rows(i) // 8)], axis=0)

    def copy(self, src, dst, sem, device):
        return remote(src, dst, self.sems.at[0, sem], self.sems.at[1, sem], device)

    def rest(self, offset, sign=1):
        x, y = self.r // 4, lax.rem(self.r, 4)
        return wrap(x + sign * offset[0], 4) * 4 + wrap(y + sign * offset[1], 4)

    def a(self):
        return self.copy(self.part.at[1 - self.c], self.ra, 0, self.other)

    def b(self, o):
        to = self.rest(o)
        k = 4 * o[0] + o[1]
        return self.copy(self.sa.at[to], self.rb.at[k], SEM_B + k, {"rest": to})

    def along(self, d):
        return self.copy(self.own, self.rz.at[self.z], SEM_Z + d, {"fibre": wrap(self.z + d, NZ) * 2 + self.c})

    def e(self, o):
        mine = self.full.at[self.c, self.r]
        return self.copy(mine, mine, SEM_E + 4 * o[0] + o[1], {"rest": self.rest(o)})

    def start(self):
        self.send(self.a())

    def spread(self):
        self.a().wait_recv()
        self.sa[...] = self.part[self.c] + self.ra[...]
        for o in ACROSS:
            self.send(self.b(o))

    def up(self):
        total = self.sa[self.r]
        for o in ACROSS:
            self.b(o).wait_recv()
            total = total + self.rb[4 * o[0] + o[1]]
        self.own[...] = total
        self.rz[self.z] = total
        for d in (4, 3, 5, 2, 6, 1, 7):
            self.send(self.along(d))

    def back(self):
        for d in range(1, NZ):
            self.along(d).wait_recv()
        s = [self.rz[k] for k in range(NZ)]
        self.full[self.c, self.r] = ((s[0] + s[1]) + (s[2] + s[3])) + ((s[4] + s[5]) + (s[6] + s[7]))
        for o in ACROSS:
            self.send(self.e(o))

    def finish(self):
        for o in ACROSS:
            self.e(o).wait_recv()
        half = self.full.at[self.c]
        copy = self.copy(half, half, SEM_F, self.other)
        self.send(copy)
        copy.wait_recv()


def main_kernel(slab, start, factor, core, fc, fh, fl, tail, tail_out, tail_in, gh, gl, basis, ahead, turned, core_tiles,
                s_own, s_x, r_x, s_z, r_z, s_o, s_sum, *sum_refs):
    f = lax.axis_index("fibre")
    r = lax.axis_index("rest")
    z = f // 2
    c = lax.rem(f, 2)

    sent = []

    def send(copy):
        copy.start()
        sent.append(copy)

    barrier = pltpu.get_barrier_semaphore()
    for d in range(1, NF):
        mesh_signal(barrier, {"fibre": wrap(f + d, NF)})
    for d in range(1, NR):
        mesh_signal(barrier, {"rest": wrap(r + d, NR)})

    sets = [(0, 16, 0), (16, 16, ROW_B), (32, 8, ROW_C)]

    def partner(o):
        dz, dc = o
        return wrap(z + dz, NZ) * 2 + (c if dc == 0 else 1 - c)

    def piece(k, to):
        at, rows, _ = sets[k]
        return slab.at[pl.ds(at, rows), pl.ds(pl.multiple_of(to * OWN, OWN), OWN)]

    def place(k):
        _, rows, base = sets[k]
        return fc.at[pl.ds(pl.multiple_of(base + f * rows, rows), rows), :]

    def x_copy(k, o):
        to = partner(o)
        n = 2 * o[0] + o[1]
        return remote(piece(k, to), place(k), s_x.at[k, n], r_x.at[k, n], {"fibre": to})

    def tail_rows(ref, at):
        return ref.at[pl.ds(pl.multiple_of(at * 16, 16), 16), :]

    def t_copy(o):
        to = partner(o)
        n = 2 * o[0] + o[1]
        return remote(tail_rows(tail_out, to), tail_rows(tail_in, f), s_x.at[3, n], r_x.at[3, n], {"fibre": to})

    tail_copy = pltpu.make_async_copy(slab.at[pl.ds(40, 2), :], tail.at[pl.ds(0, 2), :], s_own.at[3])
    tail_copy.start()
    own_copies = [pltpu.make_async_copy(piece(k, f), place(k), s_own.at[k]) for k in range(3)]
    for copy in own_copies:
        copy.start()
    pl.semaphore_wait(barrier, NF - 1 + NR - 1)

    for o in ALONG_Z:
        send(x_copy(0, o))
    for k in (1, 2):
        for o in ALONG_Z:
            send(x_copy(k, o))
    tail_copy.wait()
    for to in range(NF):
        for k in range(8):
            tail_out[pl.ds(to * 16 + k, 2, stride=8), :] = tail[0:2, pl.ds((to * 8 + k) * 128, 128)]
    tail_rows(tail_in, f)[...] = tail_rows(tail_out, f)[...]
    for o in ALONG_Z:
        send(t_copy(o))

    sums = [Sum(k, sum_refs[7 * k:7 * k + 7], s_sum, send, f, r) for k in range(4)]

    def rounded(top, rows):
        at = pl.ds(top, rows)
        fh[at, :], fl[at, :] = split(fc[at, :])

    def pair(top, rows):
        return fh[pl.ds(top, rows), :], fl[pl.ds(top, rows), :]

    def wait_set(k):
        own_copies[k].wait()
        for o in ALONG_Z:
            x_copy(k, o).wait_recv()

    def put(batch, i0, value, j0=0):
        step = block_rows(i0)
        for i, j in BATCHES[batch]:
            top, left = (i - i0) * step, (j - j0) * 128
            if 0 <= top < value.shape[0] and 0 <= left < value.shape[1] and (i == 5) == (i0 == 5):
                sums[batch].put(i, j, value[top:top + step, left:left + 128])

    def unpack(batch):
        for i, j in BATCHES[batch]:
            value = sums[batch].get(i, j)
            if i == 5:
                value = jnp.concatenate([value, jnp.zeros((96, 128), F32)], axis=0)
            for at, v in [((i, j), value)] + ([((j, i), value.T)] if i != j else []):
                where = (pl.ds(at[0] * 128, 128), pl.ds(at[1] * 128, 128))
                gh[where], gl[where] = split(v)

    fc[pl.ds(I1, PAD1 - I1), :] = jnp.zeros((PAD1 - I1, OWN), F32)
    wide_start = jnp.concatenate([start[...], jnp.zeros((RANK, PAD1 - I1), F32)], axis=1)
    basis[...] = permuted(wide_start, permutation(False))

    wait_set(0)
    rounded(0, 256)
    put(0, 0, dot3(pair(0, 256), pair(0, 256), NT))
    sums[0].start()
    sums[0].spread()
    sums[0].up()

    wait_set(1)
    rounded(ROW_B, 256)
    put(1, 2, dot3(pair(ROW_B, 256), pair(0, 512), NT))
    sums[1].start()
    sums[1].spread()
    sums[1].up()

    wait_set(2)
    rounded(ROW_C, 128)
    put(2, 4, dot3(pair(ROW_C, 128), pair(0, 640), NT))
    sums[2].start()
    sums[2].spread()

    for o in ALONG_Z:
        t_copy(o).wait_recv()
    for i in range(2):
        for k in range(8):
            fc[pl.ds(ROW_T + 16 * i, 16), pl.ds(128 * k, 128)] = tail_in[pl.ds(8 * i + k, 16, stride=16), :]
    rounded(ROW_T, PAD1 - ROW_T)
    put(3, 5, dot3(pair(ROW_T, 32), pair(0, PAD1), NT))
    sums[3].start()
    sums[3].spread()
    sums[0].back()
    sums[2].up()
    sums[1].back()
    sums[3].up()
    sums[2].back()
    sums[3].back()
    sums[0].finish()
    sums[1].finish()
    unpack(0)
    unpack(1)
    sums[2].finish()
    unpack(2)
    sums[3].finish()
    unpack(3)

    def exact(u, v):
        return lax.dot_general(u, v, NN, precision=HP, preferred_element_type=F32)

    def beside_factor(high, low, width):
        image = basis[...]
        parts = split(image)
        wide = jnp.concatenate([image, jnp.zeros((128 - RANK, PAD1), F32)], axis=0)
        small = lax.dot_general(image, wide, NT, precision=HP, preferred_element_type=F32)

        def piece(at):
            def work():
                ahead[:, at] = dot3(parts, (high[:, at], low[:, at]), NN)
            return work

        work = [piece(pl.ds(k, 256)) for k in range(0, width, 256)]
        return inverse_factor(small, work)[:, :RANK]

    basis[...] = dot3(split(basis[...]), (gh[...], gl[...]), NN)

    def step(_, carry):
        inverse = beside_factor(gh, gl, PAD1)
        basis[...] = exact(inverse, ahead[:, pl.ds(0, PAD1)])
        return carry

    lax.fori_loop(0, ITERS - 1, step, 0)
    inverse = beside_factor(fh, fl, OWN)

    product = exact(inverse, ahead[...])
    for k in range(8):
        core_tiles[pl.ds(k, RANK, stride=8), :] = product[:, 128 * k:128 * k + 128]

    def z_copy(o):
        to = partner(o)
        n = 2 * o[0] + o[1]
        return remote(core_tiles.at[pl.ds(pl.multiple_of(to * 48, 8), 48), :],
                      core.at[pl.ds(pl.multiple_of(f * 48, 8), 48), :],
                      s_z.at[n], r_z.at[n], {"fibre": to})

    for o in ALONG_Z:
        send(z_copy(o))
    own_at = pl.ds(pl.multiple_of(f * 48, 8), 48)
    core_copy = pltpu.make_async_copy(core_tiles.at[own_at, :], core.at[own_at, :], s_o.at[0])
    core_copy.start()
    turned[...] = permuted(exact(inverse, basis[...]), permutation(True))[:, :I1]
    factor_copy = pltpu.make_async_copy(turned, factor, s_o.at[1])
    factor_copy.start()

    for o in ALONG_Z:
        z_copy(o).wait_recv()
    for copy in sent:
        copy.wait_send()
    core_copy.wait()
    factor_copy.wait()


def main_call(slab, start):
    dma = pltpu.SemaphoreType.DMA
    any_spec = pl.BlockSpec(memory_space=pl.ANY)

    def tiles(*shape):
        return pltpu.VMEM((*shape, 8, 128), F32)

    sum_scratch = []
    for n in SLOTS:
        sum_scratch += [tiles(2, NR, n), tiles(NR, n), tiles(NR, n), tiles(NR, n), tiles(n), tiles(NZ, n), tiles(2, NR, n)]
    return pl.pallas_call(
        main_kernel,
        out_shape=(
            jax.ShapeDtypeStruct((RANK, I1), F32),
            jax.ShapeDtypeStruct((RANK * 8, 128), F32),
        ),
        in_specs=[any_spec, pl.BlockSpec(memory_space=pltpu.VMEM)],
        out_specs=(any_spec, any_spec),
        scratch_shapes=[
            pltpu.VMEM((PAD1, OWN), F32),
            pltpu.VMEM((PAD1, OWN), BF16),
            pltpu.VMEM((PAD1, OWN), BF16),
            pltpu.VMEM((8, COLS), F32),
            pltpu.VMEM((NF * 16, 128), F32),
            pltpu.VMEM((NF * 16, 128), F32),
            pltpu.VMEM((PAD1, PAD1), BF16),
            pltpu.VMEM((PAD1, PAD1), BF16),
            pltpu.VMEM((RANK, PAD1), F32),
            pltpu.VMEM((RANK, OWN), F32),
            pltpu.VMEM((RANK, I1), F32),
            pltpu.VMEM((RANK * 8, 128), F32),
            dma((4,)),
            dma((4, NF)), dma((4, NF)),
            dma((NF,)), dma((NF,)),
            dma((2,)),
            dma((4, 2, SEMS)),
        ] + sum_scratch,
        compiler_params=pltpu.CompilerParams(
            collective_id=0, has_side_effects=True, vmem_limit_bytes=VMEM_LIMIT),
        name="main",
    )(slab, start)


def layout_kernel(turned, tiles, factor, core):
    factor[...] = turned[...]
    for s in range(NF):
        for k in range(8):
            core[:, pl.ds((8 * s + k) * 128, 128)] = tiles[pl.ds(48 * s + k, RANK // NF, stride=8), :]


def layout_call(turned, tiles):
    vmem = pl.BlockSpec(memory_space=pltpu.VMEM)
    return pl.pallas_call(
        layout_kernel,
        out_shape=(
            jax.ShapeDtypeStruct((RANK, I1), F32),
            jax.ShapeDtypeStruct((RANK // NF, COLS), F32),
        ),
        in_specs=[vmem, vmem],
        out_specs=(vmem, vmem),
        compiler_params=pltpu.CompilerParams(vmem_limit_bytes=VMEM_LIMIT),
        name="layout",
    )(turned, tiles)


def shards(slab, start_basis):
    factor, core = layout_call(*main_call(slab, start_basis.T))
    return factor.T, core


def solution(mesh):
    return jax.shard_map(
        shards,
        mesh=mesh,
        in_specs=(P("fibre", "rest"), P()),
        out_specs=(P(), P("fibre", "rest")),
        check_vma=False,
    )
```
